256 devices in a mesh: narrow: 4 (over z_lo, core), wide: 64 (over z_hi, x, y).
Axes of the slice: x: 4, y: 4, z: 8 (z_hi: 4, z_lo: 2; z = z_hi * 2 + z_lo), core: 2. Of those that a mesh axis runs over, the one named last changes fastest.
Arguments:
- tokens: bfloat16 [512, 16384], P('narrow', 'wide'), may hold values from -6 to 6
- w_query: bfloat16 [16384, 8192], P('wide', 'narrow'), may hold values from -0.046875 to 0.046875
- w_keyval: bfloat16 [16384, 1024], P('wide', 'narrow'), may hold values from -0.046875 to 0.046875
- w_output: bfloat16 [8192, 16384], P('narrow', 'wide'), may hold values from -0.0625 to 0.0625
- grad_out: bfloat16 [512, 16384], P('narrow', 'wide'), may hold values from -6 to 6
Outputs:
- output: bfloat16 [512, 16384], P('narrow', 'wide')
- grad_tokens: bfloat16 [512, 16384], P('narrow', 'wide')
- grad_wq: bfloat16 [16384, 8192], P('wide', 'narrow')
- grad_wkv: bfloat16 [16384, 1024], P('wide', 'narrow')
- grad_wo: bfloat16 [8192, 16384], P('narrow', 'wide')
The draws below stay inside these ranges and needn't reach their ends.
All inputs are finite; a program needn't handle non-finite values.
Results may differ from the reference program's by a relative error of at most 0.015.
Values may be sent and summed in bfloat16 or wider, within the bound.
A program may use at most 64 MiB of HBM per device.

```python
import jax
import jax.numpy as jnp
from jax import lax

D = 16384
H = 64
KVH = 4
HD = 128
TOKENS = 512


def shard_levels(own_key, dims, split, smallest, top_value):
    level = 1.0
    for dim, blocks in split:
        draws = jax.random.uniform(jax.random.fold_in(jax.random.fold_in(own_key, 6), dim), (blocks,), jnp.float32, smallest / len(split), top_value / len(split))
        level = level * jnp.repeat(jnp.exp(draws), dims[dim] // blocks).reshape((-1,) + (1,) * (len(dims) - 1 - dim))
    return level


def bell_draw(rng, shape, deviation, limit, split=(), dtype=jnp.bfloat16):
    factor_of = shard_levels(rng, shape, split, -0.22, 0.18) if split else 1.0
    result = jax.random.normal(rng, shape, jnp.float32) * deviation * factor_of
    return jnp.minimum(jnp.maximum(result, -limit), limit).astype(dtype)


def setup_inputs(seed: int = 0) -> dict:
    keys = jax.random.split(jax.random.key(seed), 6)
    return {
        "tokens": bell_draw(keys[0], (TOKENS, D), 1.0, 6.0, ((0, 4), (1, 64))),
        "w_query": bell_draw(keys[1], (D, H * HD), D ** -0.5, 0.046875, ((0, 64), (1, 4))),
        "w_keyval": bell_draw(keys[2], (D, 2 * KVH * HD), D ** -0.5, 0.046875, ((0, 64), (1, 4))),
        "w_output": bell_draw(keys[3], (H * HD, D), (H * HD) ** -0.5, 0.0625, ((0, 4), (1, 64))),
        "grad_out": bell_draw(keys[4], (TOKENS, D), 1.0, 6.0, ((0, 4), (1, 64))),
    }


def round_keep(value):
    return lax.optimization_barrier(value.astype(jnp.bfloat16)).astype(jnp.float32)


def reference(tokens, w_query, w_keyval, w_output, grad_out):
    group_size = H // KVH
    score_scale = HD ** -0.5
    queries = jnp.dot(tokens, w_query, preferred_element_type=jnp.float32).astype(jnp.bfloat16)
    keyval = jnp.dot(tokens, w_keyval, preferred_element_type=jnp.float32).astype(jnp.bfloat16)
    grad_att = jnp.dot(grad_out, w_output.T, preferred_element_type=jnp.float32).astype(jnp.bfloat16)
    query_groups = queries.astype(jnp.float32).reshape(TOKENS, KVH, group_size, HD).transpose(1, 2, 0, 3)
    pair_groups = keyval.astype(jnp.float32).reshape(TOKENS, KVH, 2, HD).transpose(1, 2, 0, 3)
    grad_groups = grad_att.astype(jnp.float32).reshape(TOKENS, KVH, group_size, HD).transpose(1, 2, 0, 3)
    position = jnp.arange(TOKENS)
    allowed = position[None, :] <= position[:, None]

    def one_group(inputs):
        query_group, pair_block, grad_group = inputs
        key_block = pair_block[0]
        value_block = pair_block[1]
        scores = jnp.einsum("gtd,sd->gts", query_group, key_block) * score_scale
        weights = jnp.where(allowed[None], jnp.exp(scores), 0.0)
        weights = weights / jnp.sum(weights, axis=2, keepdims=True)
        prob_bf = round_keep(weights)
        attended = jnp.einsum("gts,sd->gtd", prob_bf, value_block)
        prob_grad = jnp.einsum("gtd,sd->gts", grad_group, value_block)
        grad_values = jnp.einsum("gts,gtd->sd", prob_bf, grad_group)
        score_grad = weights * (prob_grad - jnp.sum(weights * prob_grad, axis=2, keepdims=True))
        score_half = round_keep(score_grad)
        grad_query = jnp.einsum("gts,sd->gtd", score_half, key_block) * score_scale
        grad_keys = jnp.einsum("gts,gtd->sd", score_half, query_group) * score_scale
        return attended, grad_query, jnp.stack([grad_keys, grad_values], axis=0)

    attended_all, grad_q_all, grad_pairs = lax.map(one_group, (query_groups, pair_groups, grad_groups))
    attended = attended_all.transpose(2, 0, 1, 3).reshape(TOKENS, H * HD).astype(jnp.bfloat16)
    grad_q = grad_q_all.transpose(2, 0, 1, 3).reshape(TOKENS, H * HD).astype(jnp.bfloat16)
    grad_kv = grad_pairs.transpose(2, 0, 1, 3).reshape(TOKENS, 2 * KVH * HD).astype(jnp.bfloat16)
    output = jnp.dot(attended, w_output, preferred_element_type=jnp.float32).astype(jnp.bfloat16)
    grad_wo = jnp.dot(attended.T, grad_out, preferred_element_type=jnp.float32).astype(jnp.bfloat16)
    grad_mixed = jnp.concatenate([grad_q, grad_kv], axis=1)
    grad_joined = jnp.dot(tokens.T, grad_mixed, preferred_element_type=jnp.float32)
    grad_wq = grad_joined[:, :H * HD].astype(jnp.bfloat16)
    grad_wkv = grad_joined[:, H * HD:].astype(jnp.bfloat16)
    joined = jnp.concatenate([w_query, w_keyval], axis=1)
    grad_tokens = jnp.dot(grad_mixed, joined.T, preferred_element_type=jnp.float32).astype(jnp.bfloat16)
    return (output, grad_tokens, grad_wq, grad_wkv, grad_wo)
```

```python
import functools

import jax
import jax.numpy as jnp
from jax import lax
from jax.experimental import pallas as pl
from jax.experimental.pallas import tpu as pltpu
from jax.sharding import PartitionSpec as P

HD = 128
F32 = jnp.float32
BF16 = jnp.bfloat16
MESH = pl.DeviceIdType.MESH
SEMS = 160


def mm(left, right, dims):
    return lax.dot_general(left, right, (dims, ((), ())), preferred_element_type=F32)


NN = ((1,), (0,))
NT = ((1,), (1,))
TN = ((0,), (0,))


def kernel(
    K, N, tok, wq_h, wkv_h, wo_h, gout,
    out_h, gtok_h, gwq_h, gwkv_h, gwo_h,
    wq, wkv, wo, tpan, gpan, pq, pg, pkv, pkg,
    q1, qs1, q2, qs2, q3, qf,
    g1, gs1, g2, gs2, g3, gf,
    k1, ks1, k2, ks2, k3,
    m1, ms1, m2, ms2, m3,
    kvp, kgp, ap, dp, o_part, o_recv, t_part, t_recv,
    o_out, t_out, gwq_o, gwkv_o, gwo_o,
    send_sems, recv_sems, local_sems,
):
    Z = K
    R, U = pq.shape[3], pq.shape[4]
    rows = K * K * R
    C = 2 * Z
    me = lax.axis_index("wide")
    nar = lax.axis_index("narrow")
    z, x, y = me // (K * K), (me // K) % K, me % K
    part_rows = rows // N

    def peer(axis, d):
        if axis == "n":
            i = (nar + d) % N
            return {"narrow": i}, i
        if axis == "z":
            i = (z + d) % K
            return {"wide": i * K * K + x * K + y}, i
        if axis == "x":
            i = (x + d) % K
            return {"wide": z * K * K + i * K + y}, i
        i = (y + d) % K
        return {"wide": z * K * K + x * K + i}, i

    count = [0]
    sent = []

    def send(axis, src, dst):
        copies = []
        for d in range(1, N if axis == "n" else K):
            device, place = peer(axis, d)
            i = count[0]
            count[0] += 1
            c = pltpu.make_async_remote_copy(
                src_ref=src(place), dst_ref=dst(d),
                send_sem=send_sems.at[i], recv_sem=recv_sems.at[i],
                device_id=device, device_id_type=MESH,
            )
            c.start()
            copies.append(c)
        sent.extend(copies)
        return copies

    def arrived(copies):
        for c in copies:
            c.wait_recv()

    loads = []
    for i, (s, d) in enumerate(
        [(tok, tpan.at[nar]), (gout, gpan.at[nar]), (wkv_h, wkv), (wq_h, wq), (wo_h, wo)]
    ):
        c = pltpu.make_async_copy(s, d, local_sems.at[i])
        c.start()
        loads.append(c)

    barrier = pltpu.get_barrier_semaphore()
    peers = [("n", d) for d in range(1, N)] + [(a, d) for a in "zxy" for d in range(1, K)]
    for a, d in peers:
        pl.semaphore_signal(barrier, inc=1, device_id=peer(a, d)[0], device_id_type=MESH)
    pl.semaphore_wait(barrier, len(peers))

    tok_c = send("n", lambda p: tok, lambda d: tpan.at[nar])
    gout_c = send("n", lambda p: gout, lambda d: gpan.at[nar])

    first = ("x", "y")
    second = ("y", "x")

    def rs_send1(p, recv, h, per):
        u = slice(h * per, (h + 1) * per)
        if h == 0:
            return send("x", lambda i: p.at[u, i], lambda d: recv.at[h, d - 1])
        return send("y", lambda i: p.at[u, :, i], lambda d: recv.at[h, d - 1])

    def rs_sum1(p, recv, s, h, per):
        def body(u, _):
            own = p[h * per + u, x] if h == 0 else p[h * per + u, :, y]
            total = own.astype(F32)
            for d in range(K - 1):
                total += recv[h, d, u].astype(F32)
            s[h, u] = total.astype(BF16)
            return 0

        lax.fori_loop(0, per, body, 0)

    def rs_send2(s, recv, h):
        return send(second[h], lambda i: s.at[h, :, i], lambda d: recv.at[h, d - 1])

    def rs_sum2(s, recv, t, h):
        own = s[h, :, y] if h == 0 else s[h, :, x]
        total = own.astype(F32)
        for d in range(K - 1):
            total += recv[h, d].astype(F32)
        t[h] = total.astype(BF16)

    def ag_send2(p, h, per):
        here = p.at[h * per:(h + 1) * per, x, y]
        return send(second[h], lambda i: here, lambda d: here)

    def ag_send3(p, h, per):
        u = slice(h * per, (h + 1) * per)
        here = p.at[u, x] if h == 0 else p.at[u, :, y]
        return send(first[h], lambda i: here, lambda d: here)

    both = (0, 1)

    arrived(tok_c)
    for i in (0, 2, 3):
        loads[i].wait()
    tokens = tpan[...].reshape(rows, -1)
    kv = mm(tokens, wkv[...], NN).astype(BF16)
    for h in both:
        pkv[h] = kv[:, h * HD:(h + 1) * HD].reshape(K, K, R, HD)
    k1_c = [rs_send1(pkv, k1, h, 1) for h in both]
    q1_c = []
    for h in both:
        for c in range(h * Z, (h + 1) * Z):
            pq[c] = mm(tokens, wq[:, c * U:(c + 1) * U], NN).astype(BF16).reshape(K, K, R, U)
        q1_c.append(rs_send1(pq, q1, h, Z))
    arrived(gout_c)
    for i in (1, 4):
        loads[i].wait()
    grads = gpan[...].reshape(rows, -1)
    g1_c = []
    for h in both:
        for c in range(h * Z, (h + 1) * Z):
            pg[c] = mm(grads, wo[c * U:(c + 1) * U, :], NT).astype(BF16).reshape(K, K, R, U)
        g1_c.append(rs_send1(pg, g1, h, Z))

    k2_c = []
    for h in both:
        arrived(k1_c[h])
        rs_sum1(pkv, k1, ks1, h, 1)
        k2_c.append(rs_send2(ks1, k2, h))
    q2_c = []
    for h in both:
        arrived(q1_c[h])
        rs_sum1(pq, q1, qs1, h, Z)
        q2_c.append(rs_send2(qs1, q2, h))

    def share_z(s, recv, h):
        return send("z", lambda i: s.at[h], lambda d: recv.at[h, d - 1])

    def finish_shared(s, recv, p, h):
        total = s[h].astype(F32)
        for d in range(K - 1):
            total += recv[h, d].astype(F32)
        p[h, x, y] = total.astype(BF16)[0]

    def rs_send3(s, recv, h):
        return send("z", lambda i: s.at[h, i], lambda d: recv.at[h, d - 1])

    def rs_finish(s, recv, f, h):
        total = s[h, z].astype(F32)
        for d in range(K - 1):
            total += recv[h, d].astype(F32)
        f[h] = total.astype(BF16)

    k3_c = []
    for h in both:
        arrived(k2_c[h])
        rs_sum2(ks1, k2, ks2, h)
        k3_c.append(share_z(ks2, k3, h))
    q3_c = []
    for h in both:
        arrived(q2_c[h])
        rs_sum2(qs1, q2, qs2, h)
        q3_c.append(rs_send3(qs2, q3, h))
    ka_c = []
    for h in both:
        arrived(k3_c[h])
        finish_shared(ks2, k3, kvp, h)
        ka_c.append(ag_send2(kvp, h, 1))
    kb_c = []
    for h in both:
        arrived(ka_c[h])
        kb_c.append(ag_send3(kvp, h, 1))
    for h in both:
        arrived(q3_c[h])
        rs_finish(qs2, q3, qf, h)
    for h in both:
        arrived(kb_c[h])

    def heads(f):
        return jnp.concatenate(
            [f[h, :, k * HD:(k + 1) * HD] for h in both for k in range(U // HD)], axis=0
        )

    def unheads(p, v):
        per = U // HD
        for h in both:
            p[h * Z + z, x, y] = jnp.concatenate(
                [v[(h * per + k) * R:(h * per + k + 1) * R] for k in range(per)], axis=1
            )

    scale = HD ** (-0.5)
    queries = heads(qf)
    keys = kvp[0].reshape(rows, HD)
    values = kvp[1].reshape(rows, HD)
    scores = mm(queries, keys, NT) * scale
    place = lax.broadcasted_iota(jnp.int32, scores.shape, 0) % R + (x * K + y) * R
    allowed = lax.broadcasted_iota(jnp.int32, scores.shape, 1) <= place
    weights = jnp.where(allowed, jnp.exp(scores), 0.0)
    weights = weights / jnp.sum(weights, axis=1, keepdims=True)
    probs = weights.astype(BF16)
    unheads(ap, mm(probs, values, NN).astype(BF16))

    def ag_send1(p, h):
        here = p.at[h * Z + z, x, y]
        return send("z", lambda i: here, lambda d: here)

    a1_c = [ag_send1(ap, h) for h in both]

    g2_c = []
    for h in both:
        arrived(g1_c[h])
        rs_sum1(pg, g1, gs1, h, Z)
        g2_c.append(rs_send2(gs1, g2, h))
    g3_c = []
    for h in both:
        arrived(g2_c[h])
        rs_sum2(gs1, g2, gs2, h)
        g3_c.append(rs_send3(gs2, g3, h))
    a2_c = []
    for h in both:
        arrived(a1_c[h])
        a2_c.append(ag_send2(ap, h, Z))
    for h in both:
        arrived(g3_c[h])
        rs_finish(gs2, g3, gf, h)

    cotangent = heads(gf)
    prob_grad = mm(cotangent, values, NT)
    score_grad = weights * (prob_grad - jnp.sum(weights * prob_grad, axis=1, keepdims=True))
    score_half = score_grad.astype(BF16)
    grad_keys = mm(score_half, queries, TN) * scale
    grad_values = mm(probs, cotangent, TN)
    pkg[0] = grad_keys.astype(BF16).reshape(K, K, R, HD)
    pkg[1] = grad_values.astype(BF16).reshape(K, K, R, HD)
    m1_c = [rs_send1(pkg, m1, h, 1) for h in both]
    unheads(dp, (mm(score_half, keys, NN) * scale).astype(BF16))
    d1_c = [ag_send1(dp, h) for h in both]

    m2_c = []
    for h in both:
        arrived(m1_c[h])
        rs_sum1(pkg, m1, ms1, h, 1)
        m2_c.append(rs_send2(ms1, m2, h))
    d2_c = []
    for h in both:
        arrived(d1_c[h])
        d2_c.append(ag_send2(dp, h, Z))
    m3_c = []
    for h in both:
        arrived(m2_c[h])
        rs_sum2(ms1, m2, ms2, h)
        m3_c.append(share_z(ms2, m3, h))
    a3_c = []
    for h in both:
        arrived(a2_c[h])
        a3_c.append(ag_send3(ap, h, Z))
    ma_c = []
    for h in both:
        arrived(m3_c[h])
        finish_shared(ms2, m3, kgp, h)
        ma_c.append(ag_send2(kgp, h, 1))
    d3_c = []
    for h in both:
        arrived(d2_c[h])
        d3_c.append(ag_send3(dp, h, Z))
    mb_c = []
    for h in both:
        arrived(ma_c[h])
        mb_c.append(ag_send3(kgp, h, 1))

    def unit(p, c):
        return p[c].reshape(rows, U)

    def sum_narrow(part, recv, o):
        total = part[nar].astype(F32)
        for d in range(N - 1):
            total += recv[d].astype(F32)
        o[...] = total.astype(BF16)

    stores = []

    def store(s, d):
        c = pltpu.make_async_copy(s, d, local_sems.at[5 + len(stores)])
        c.start()
        stores.append(c)

    total = None
    for h in both:
        arrived(a3_c[h])
        for c in range(h * Z, (h + 1) * Z):
            term = mm(unit(ap, c), wo[c * U:(c + 1) * U, :], NN)
            total = term if total is None else total + term
    o_part[...] = total.astype(BF16).reshape(N, part_rows, -1)
    o_c = send("n", lambda i: o_part.at[i], lambda d: o_recv.at[d - 1])
    for c in range(C):
        gwo_o[c * U:(c + 1) * U, :] = mm(unit(ap, c), grads, TN).astype(BF16)
    store(gwo_o, gwo_h)
    arrived(o_c)
    sum_narrow(o_part, o_recv, o_out)
    store(o_out, out_h)

    total = None
    for h in both:
        arrived(d3_c[h])
        for c in range(h * Z, (h + 1) * Z):
            term = mm(unit(dp, c), wq[:, c * U:(c + 1) * U], NT)
            total = term if total is None else total + term
    for h in both:
        arrived(mb_c[h])
    kv_grad = jnp.concatenate([kgp[h].reshape(rows, HD) for h in both], axis=1)
    total = total + mm(kv_grad, wkv[...], NT)
    t_part[...] = total.astype(BF16).reshape(N, part_rows, -1)
    t_c = send("n", lambda i: t_part.at[i], lambda d: t_recv.at[d - 1])
    tokens_t = tpan[...].reshape(rows, -1)
    for c in range(C):
        gwq_o[:, c * U:(c + 1) * U] = mm(tokens_t, unit(dp, c), TN).astype(BF16)
    store(gwq_o, gwq_h)
    gwkv_o[...] = mm(tokens_t, kv_grad, TN).astype(BF16)
    store(gwkv_o, gwkv_h)
    arrived(t_c)
    sum_narrow(t_part, t_recv, t_out)
    store(t_out, gtok_h)
    for c in stores:
        c.wait()
    for c in sent:
        c.wait_send()


def shards(K, N, tokens, w_query, w_keyval, w_output, grad_out):
    part_rows, feat = tokens.shape
    rows = part_rows * N
    R = rows // (K * K)
    qc = w_query.shape[1]
    Z = K
    C = 2 * Z
    U = qc // C
    assert w_keyval.shape[1] == 2 * HD and U % HD == 0

    def v(*shape):
        return pltpu.VMEM(shape, BF16)

    def reduce_buffers():
        return [
            v(2, K - 1, Z, K, R, U), v(2, Z, K, R, U), v(2, K - 1, Z, R, U), v(2, Z, R, U),
            v(2, K - 1, R, U), v(2, R, U),
        ]

    def pair_buffers():
        return [
            v(2, K - 1, 1, K, R, HD), v(2, 1, K, R, HD), v(2, K - 1, 1, R, HD), v(2, 1, R, HD),
            v(2, K - 1, 1, R, HD),
        ]

    def panel():
        return v(C, K, K, R, U)

    def pair_panel():
        return v(2, K, K, R, HD)

    scratch = (
        [v(*w_query.shape), v(*w_keyval.shape), v(*w_output.shape)]
        + [v(N, part_rows, feat), v(N, part_rows, feat)]
        + [panel(), panel(), pair_panel(), pair_panel()]
        + reduce_buffers() + reduce_buffers() + pair_buffers() + pair_buffers()
        + [pair_panel(), pair_panel(), panel(), panel()]
        + [v(N, part_rows, feat), v(N - 1, part_rows, feat)] * 2
        + [v(part_rows, feat), v(part_rows, feat)]
        + [v(*w_query.shape), v(*w_keyval.shape), v(*w_output.shape)]
        + [pltpu.SemaphoreType.DMA((SEMS,)), pltpu.SemaphoreType.DMA((SEMS,))]
        + [pltpu.SemaphoreType.DMA((10,))]
    )
    anywhere = pl.BlockSpec(memory_space=pl.ANY)
    shape = lambda a: jax.ShapeDtypeStruct(a.shape, BF16)
    return pl.pallas_call(
        functools.partial(kernel, K, N),
        out_shape=(shape(grad_out), shape(tokens), shape(w_query), shape(w_keyval), shape(w_output)),
        in_specs=[anywhere] * 5,
        out_specs=(anywhere,) * 5,
        scratch_shapes=scratch,
        compiler_params=pltpu.CompilerParams(
            collective_id=0, has_side_effects=True, vmem_limit_bytes=56 * 1024 * 1024
        ),
        name="layer",
    )(tokens, w_query, w_keyval, w_output, grad_out)


def solution(mesh):
    N, wide = mesh.shape["narrow"], mesh.shape["wide"]
    K = next(k for k in range(1, wide + 1) if k ** 3 >= wide)
    assert K ** 3 == wide
    return jax.shard_map(
        functools.partial(shards, K, N),
        mesh=mesh,
        in_specs=(
            P("narrow", "wide"),
            P("wide", "narrow"),
            P("wide", "narrow"),
            P("narrow", "wide"),
            P("narrow", "wide"),
        ),
        out_specs=(
            P("narrow", "wide"),
            P("narrow", "wide"),
            P("wide", "narrow"),
            P("wide", "narrow"),
            P("narrow", "wide"),
        ),
        check_vma=False,
    )
```

```python
import functools

import jax
import jax.numpy as jnp
from jax import lax
from jax.experimental import pallas as pl
from jax.experimental.pallas import tpu as pltpu
from jax.sharding import PartitionSpec as P

HD = 128
F32 = jnp.float32
BF16 = jnp.bfloat16
MESH = pl.DeviceIdType.MESH
RECV_SEMS = 130
SEND_SEMS = 24
LOCAL_SEMS = 26
PIECES = 4
REDUCE_GROUPS = ((0, 1), (1, 2), (2, 3), (3, 4))
GATHER_GROUPS = ((0, 1), (1, 2), (2, 3), (3, 4))


def mm(left, right, dims):
    return lax.dot_general(left, right, (dims, ((), ())), preferred_element_type=F32)


NN = ((1,), (0,))
NT = ((1,), (1,))
TN = ((0,), (0,))


def kernel(
    K, N, tok, wq_h, wkv_h, wo_h, gout,
    out_h, gtok_h, gwq_h, gwkv_h, gwo_h,
    wq, wkv, wo, tpan, gpan, pq, pg, pkv, pkg,
    q_far, q_mid, q_near, qs1, q2, qs2, q3, qf,
    g_far, g_mid, g_near, gs1, g2, gs2, g3, gf,
    k1, ks1, k2, ks2, k3,
    m1, ms1, m2, ms2, m3,
    kvp, kgp, kg, ap, dp, acc, o_part, o_recv, t_part, t_recv, o_out, t_out,
    tokens_t, gwq_o, gwkv_o, gwo_o,
    send_sems, recv_sems, local_sems,
):
    Z = K
    B = K // 2
    R, U = pq.shape[4], pq.shape[5]
    rows = K * K * R
    C = 2 * Z
    me = lax.axis_index("wide")
    nar = lax.axis_index("narrow")
    z, x, y = me // (K * K), (me // K) % K, me % K
    part_rows = rows // N
    both = (0, 1)
    first = ("x", "y")
    second = ("y", "x")
    spot = (x, y)
    low, high = slice(0, B), slice(B, K)

    def peer(axis, d):
        if axis == "core":
            i = nar + 1 - 2 * (nar % 2)
            return {"narrow": i}, i
        if axis == "n":
            i = (nar + d) % N
            return {"narrow": i}, i
        if axis == "z":
            i = (z + d) % K
            return {"wide": i * K * K + x * K + y}, i
        if axis == "x":
            i = (x + d) % K
            return {"wide": z * K * K + i * K + y}, i
        i = (y + d) % K
        return {"wide": z * K * K + x * K + i}, i

    count = [0]
    sends = []

    def receiver():
        count[0] += 1
        return count[0] - 1

    def remote(axis, d, src, dst, send_sem, recv_sem):
        return pltpu.make_async_remote_copy(
            src_ref=src, dst_ref=dst, send_sem=send_sems.at[send_sem],
            recv_sem=recv_sems.at[recv_sem], device_id=peer(axis, d)[0], device_id_type=MESH,
        )

    def wait_sent(n):
        i, ref = sends[n]
        remote("core", 1, ref, ref, i, 0).wait_send()

    def batch(items, gone):
        n = len(sends)
        if n >= SEND_SEMS:
            wait_sent(n - SEND_SEMS)
        i = n % SEND_SEMS
        sends.append((i, gone))
        for axis, d, src, dst, r in items:
            remote(axis, d, src, dst, i, r).start()

    def got(r, ref):
        remote("core", 1, ref, ref, 0, r).wait_recv()

    def fan(axis, src, dst, whole):
        r = receiver()
        ds = range(1, N if axis == "n" else K)
        batch([(axis, d, src(peer(axis, d)[1]), dst(d), r) for d in ds], whole)
        return r, whole

    locals_used = [0]

    def local(pairs):
        sem = local_sems.at[locals_used[0]]
        locals_used[0] += 1
        for s, d in pairs:
            pltpu.make_async_copy(s, d, sem).start()
        return sem

    def local_done(sem, ref):
        pltpu.make_async_copy(ref, ref, sem).wait()

    tok_l = local([(tok, tpan.at[nar])])
    gout_l = local([(gout, gpan.at[nar])])
    wkv_l = local([(wkv_h, wkv)])
    wq_l = local([(wq_h.at[:, c * U:(c + 1) * U], wq.at[c]) for c in range(C)])
    wo_l = local([(wo_h, wo)])

    barrier = pltpu.get_barrier_semaphore()
    peers = [("n", d) for d in range(1, N)] + [(a, d) for a in "zxy" for d in range(1, K)]
    for a, d in peers:
        pl.semaphore_signal(barrier, inc=1, device_id=peer(a, d)[0], device_id_type=MESH)
    pl.semaphore_wait(barrier, len(peers))

    def share_start(own, pan):
        far, near = receiver(), receiver()
        batch(
            [("n", 2, own, pan.at[nar], far), ("core", 1, own, pan.at[nar], near)], pan.at[0:2]
        )
        return far, near

    def share_end(pan, far, near):
        other = (nar + 2) % N
        got(far, pan.at[0])
        batch([("core", 1, pan.at[other], pan.at[other], near)], pan.at[0])
        got(near, pan.at[0:2])

    tok_c = share_start(tok, tpan)
    gout_c = share_start(gout, gpan)

    def small1(p, recv):
        out = []
        for h in both:
            src = (lambda i: p.at[h, i]) if h == 0 else (lambda i: p.at[h, :, i])
            out.append(fan(first[h], src, lambda d: recv.at[h, d - 1], recv.at[h]))
        return out

    def small2(waits, p, recv, s, recv2):
        out = []
        for h in both:
            got(*waits[h])
            total = (p[h, x] if h == 0 else p[h, :, y]).astype(F32)
            for d in range(K - 1):
                total += recv[h, d].astype(F32)
            s[h] = total.astype(BF16)
            out.append(fan(second[h], lambda i: s.at[h, i], lambda d: recv2.at[h, d - 1], recv2.at[h]))
        return out

    def small3(waits, s, recv2, t, recv3):
        out = []
        for h in both:
            got(*waits[h])
            total = s[h, spot[1 - h]].astype(F32)
            for d in range(K - 1):
                total += recv2[h, d].astype(F32)
            t[h] = total.astype(BF16)
            out.append(fan("z", lambda i: t.at[h], lambda d: recv3.at[h, d - 1], recv3.at[h]))
        return out

    def small4(waits, t, recv3, p):
        out = []
        for h in both:
            got(*waits[h])
            total = t[h].astype(F32)
            for d in range(K - 1):
                total += recv3[h, d].astype(F32)
            p[h, x, y] = total.astype(BF16)
            here = p.at[h, x, y]
            out.append(fan(second[h], lambda i: here, lambda d: here, p.at[h, 0, 1:K]))
        return out

    def small5(waits, p):
        out = []
        for h in both:
            got(*waits[h])
            here = p.at[h, x] if h == 0 else p.at[h, :, y]
            out.append(fan(first[h], lambda i: here, lambda d: here, p.at[h, 1:K]))
        return out

    def view(h, slots, i, part):
        return (h, slots, i, part) if h == 0 else (h, slots, part, i)

    class Reduce:
        groups = REDUCE_GROUPS

        def __init__(self, p, far, mid, near, s1, r2, s2, r3, f):
            self.p, self.far, self.mid, self.near = p, far, mid, near
            self.s1, self.r2, self.s2, self.r3, self.f = s1, r2, s2, r3, f
            self.c1, self.c2 = {}, {}
            self.c3 = receiver()

        def weight(self, h, e):
            return h * Z + (z + 1 + e) % K

        def start(self, n):
            slots = slice(*self.groups[n])
            for h in both:
                i = spot[h]
                there, after, before = (i + 2) % K, (i + 1) % K, (i + K - 1) % K
                axis, p = first[h], self.p
                f, r = receiver(), receiver()
                self.c1[n, h] = f, r
                batch([
                    (axis, 1, p.at[view(h, slots, there, low)], self.far.at[h, 0, slots], f),
                    (axis, K - 1, p.at[view(h, slots, there, high)], self.far.at[h, 1, slots], f),
                    (axis, 1, p.at[view(h, slots, after, high)], self.near.at[h, 0, slots, high], r),
                    (axis, K - 1, p.at[view(h, slots, before, low)], self.near.at[h, 1, slots, low], r),
                ], self.near.at[h, :, slots])

        def relay(self, n):
            slots = slice(*self.groups[n])
            for h in both:
                i = spot[h]
                f, r = self.c1[n, h]
                got(f, self.far.at[h, :, slots])
                items = []
                for side, d, part in ((0, 1, low), (1, K - 1, high)):
                    for e in range(*self.groups[n]):
                        own = self.p[view(h, e, (i + d) % K, part)].astype(F32)
                        total = own + self.far[h, side, e].astype(F32)
                        self.mid[h, side, e] = total.astype(BF16)
                    items.append((
                        first[h], d, self.mid.at[h, side, slots],
                        self.near.at[h, side, slots, part], r,
                    ))
                batch(items, self.mid.at[h, :, slots])

        def collect(self, n):
            slots = slice(*self.groups[n])
            for h in both:
                got(self.c1[n, h][1], self.near.at[h, :, slots])
                for e in range(*self.groups[n]):
                    total = self.p[view(h, e, spot[h], slice(0, K))].astype(F32)
                    total += self.near[h, 0, e].astype(F32)
                    total += self.near[h, 1, e].astype(F32)
                    self.s1[h, e] = total.astype(BF16)
                self.c2[n, h] = fan(
                    second[h], lambda i: self.s1.at[h, slots, i],
                    lambda d: self.r2.at[h, d - 1, slots], self.r2.at[h, :, slots],
                )

        def across(self, n):
            for h in both:
                got(*self.c2[n, h])
                for e in range(*self.groups[n]):
                    total = self.s1[h, e, spot[1 - h]].astype(F32)
                    for d in range(K - 1):
                        total += self.r2[h, d, e].astype(F32)
                    self.s2[h, e] = total.astype(BF16)
            items = [
                ("z", e + 1, self.s2.at[:, e], self.r3.at[e], self.c3)
                for e in range(*self.groups[n]) if e < K - 1
            ]
            if items:
                batch(items, self.r3.at[0:len(items)])

        def finish(self):
            got(self.c3, self.r3)
            total = self.s2[:, K - 1].astype(F32)
            for d in range(K - 1):
                total += self.r3[d].astype(F32)
            self.f[...] = total.astype(BF16)

    class Gather:
        groups = GATHER_GROUPS

        def __init__(self, p):
            self.p = p
            self.c1, self.c2, self.c3, self.c4 = [], {}, {}, {}

        def weight(self, h, e):
            return h * Z + (z + K - e) % K

        def start(self):
            p = self.p
            self.c1 = [receiver() for d in range(1, K)]
            batch(
                [("z", d, p.at[:, 0, x, y], p.at[:, d, x, y], self.c1[d - 1]) for d in range(1, K)],
                p.at[:, 1:K, 0, 0],
            )

        def across(self, n):
            e0, e1 = self.groups[n]
            for e in range(max(e0, 1), e1):
                got(self.c1[e - 1], self.p.at[:, e, 0, 0])
            for h in both:
                here = self.p.at[h, e0:e1, x, y]
                self.c2[n, h] = fan(
                    second[h], lambda i: here, lambda d: here, self.p.at[h, e0:e1, 0, 1:K]
                )

        def ring(self, n):
            slots = slice(*self.groups[n])
            for h in both:
                got(*self.c2[n, h])
                here = self.p.at[view(h, slots, spot[h], slice(0, K))]
                r = receiver()
                self.c3[n, h] = r
                batch([(first[h], d, here, here, r) for d in (1, K - 1)], self.p.at[h, slots, 0:2])

        def relay(self, n):
            slots = slice(*self.groups[n])
            for h in both:
                got(self.c3[n, h], self.p.at[h, slots, 0:2])
                r = receiver()
                self.c4[n, h] = r
                items = []
                for d, part in ((1, low), (K - 1, high)):
                    here = self.p.at[view(h, slots, (spot[h] + K - d) % K, part)]
                    items.append((first[h], d, here, here, r))
                batch(items, self.p.at[h, slots, 0])

        def done(self, n):
            slots = slice(*self.groups[n])
            for h in both:
                got(self.c4[n, h], self.p.at[h, slots, 0])

    def tall(pan):
        return pan[...].reshape(rows, -1)

    local_done(tok_l, tok)
    share_end(tpan, *tok_c)
    local_done(wkv_l, wkv)
    kv = mm(tall(tpan), wkv[...], NN).astype(BF16)
    for h in both:
        pkv[h] = kv[:, h * HD:(h + 1) * HD].reshape(K, K, R, HD)
    k_c = small1(pkv, k1)
    local_done(wq_l, wq)

    q = Reduce(pq, q_far, q_mid, q_near, qs1, q2, qs2, q3, qf)
    g = Reduce(pg, g_far, g_mid, g_near, gs1, g2, gs2, g3, gf)

    def project(n):
        for e in range(*q.groups[n]):
            for h in both:
                v = mm(tall(tpan), wq[q.weight(h, e)], NN)
                pq[h, e] = v.astype(BF16).reshape(K, K, R, U)

    def back_out(n):
        for e in range(*g.groups[n]):
            for h in both:
                at = pl.multiple_of(g.weight(h, e) * U, U)
                v = mm(tall(gpan), wo[pl.ds(at, U), :], NT)
                pg[h, e] = v.astype(BF16).reshape(K, K, R, U)

    G = len(REDUCE_GROUPS)
    work = [(q, n) for n in range(G)] + [(g, n) for n in range(G)]

    def step(t):
        if t < 2 * G:
            s, n = work[t]
            (project if s is q else back_out)(n)
            s.start(n)
        for lag, name in ((1, "relay"), (2, "collect"), (3, "across")):
            if 0 <= t - lag < 2 * G:
                s, n = work[t - lag]
                getattr(s, name)(n)

    def g_ready():
        share_end(gpan, *gout_c)
        local_done(gout_l, gout)
        local_done(wo_l, wo)

    def heads(f):
        return jnp.concatenate(
            [f[h, :, k * HD:(k + 1) * HD] for h in both for k in range(U // HD)], axis=0
        )

    def unheads(p, v):
        per = U // HD
        for h in both:
            p[h, 0, x, y] = jnp.concatenate(
                [v[(h * per + k) * R:(h * per + k + 1) * R] for k in range(per)], axis=1
            )

    scale = HD ** (-0.5)
    kept = {}

    def output_end():
        got(*kept["o"])
        sum_narrow(o_part, o_recv, o_out)
        store([(o_out, out_h)], o_out)

    def forward():
        q.finish()
        for h in both:
            got(*kept["k"][h])
        queries = heads(qf)
        keys = kvp[0].reshape(rows, HD)
        values = kvp[1].reshape(rows, HD)
        scores = mm(queries, keys, NT) * scale
        place = lax.broadcasted_iota(jnp.int32, scores.shape, 0) % R + (x * K + y) * R
        allowed = lax.broadcasted_iota(jnp.int32, scores.shape, 1) <= place
        weights = jnp.where(allowed, jnp.exp(scores), 0.0)
        weights = weights / jnp.sum(weights, axis=1, keepdims=True)
        probs = weights.astype(BF16)
        unheads(ap, mm(probs, values, NN).astype(BF16))
        kept["fwd"] = queries, keys, values, weights, probs

    def backward():
        g.finish()
        queries, keys, values, weights, probs = kept["fwd"]
        cotangent = heads(gf)
        prob_grad = mm(cotangent, values, NT)
        score_grad = weights * (prob_grad - jnp.sum(weights * prob_grad, axis=1, keepdims=True))
        score_half = score_grad.astype(BF16)
        unheads(dp, (mm(score_half, keys, NN) * scale).astype(BF16))
        dq.start()
        dq.across(0)
        grad_keys = mm(score_half, queries, TN) * scale
        grad_values = mm(probs, cotangent, TN)
        pkg[0] = grad_keys.astype(BF16).reshape(K, K, R, HD)
        pkg[1] = grad_values.astype(BF16).reshape(K, K, R, HD)
        kept["m"] = small1(pkg, m1)

    att = Gather(ap)
    dq = Gather(dp)
    stores = []

    def store(pairs, ref):
        stores.append((local(pairs), ref))

    def sum_narrow(part, recv, o):
        total = part[nar].astype(F32)
        for d in range(N - 1):
            total += recv[d].astype(F32)
        o[...] = total.astype(BF16)

    def w_output_grad(n):
        for e in range(*att.groups[n]):
            for h in both:
                c = att.weight(h, e)
                gwo_o[h, e] = mm(ap[h, e].reshape(rows, U), tall(gpan), TN).astype(BF16)
                store([(gwo_o.at[h, e], gwo_h.at[pl.ds(pl.multiple_of(c * U, U), U), :])], gwo_o.at[h, e])

    def w_query_grad(n):
        for e in range(*dq.groups[n]):
            for h in both:
                c = dq.weight(h, e)
                gwq_o[h, e] = mm(tokens_t[...], dp[h, e].reshape(rows, U), NN).astype(BF16)
                store([(gwq_o.at[h, e], gwq_h.at[:, pl.ds(pl.multiple_of(c * U, U), U)])], gwq_o.at[h, e])

    def add(term, start=False):
        acc[...] = term if start else acc[...] + term

    def output_part(n):
        for e in range(*att.groups[n]):
            for h in both:
                at = pl.multiple_of(att.weight(h, e) * U, U)
                add(mm(ap[h, e].reshape(rows, U), wo[pl.ds(at, U), :], NN), e == 0 and h == 0)

    def output_send():
        o_part[...] = acc[...].astype(BF16).reshape(N, part_rows, -1)
        kept["o"] = fan("n", lambda i: o_part.at[i], lambda d: o_recv.at[d - 1], o_recv)

    def kv_grad_part():
        for h in both:
            got(*kept["m"][h])
        kg[...] = jnp.concatenate([kgp[h].reshape(rows, HD) for h in both], axis=1)
        gwkv_o[...] = mm(tokens_t[...], kg[...], NN).astype(BF16)
        store([(gwkv_o, gwkv_h)], gwkv_o)
        add(mm(kg[...], wkv[...], NT), True)

    def token_grad_part(n):
        for e in range(*dq.groups[n]):
            for h in both:
                add(mm(dp[h, e].reshape(rows, U), wq[dq.weight(h, e)], NT))

    def m_2():
        kept["m"] = small2(kept["m"], pkg, m1, ms1, m2)

    def m_3():
        kept["m"] = small3(kept["m"], ms1, m2, ms2, m3)

    def m_4():
        kept["m"] = small4(kept["m"], ms2, m3, kgp)

    def m_5():
        kept["m"] = small5(kept["m"], kgp)

    def k_2():
        kept["k"] = small2(k_c, pkv, k1, ks1, k2)

    def k_3():
        kept["k"] = small3(kept["k"], ks1, k2, ks2, k3)

    def k_4():
        kept["k"] = small4(kept["k"], ks2, k3, kvp)

    def k_5():
        kept["k"] = small5(kept["k"], kvp)

    step(0)
    step(1)
    k_2()
    step(2)
    k_3()
    step(3)
    k_4()
    g_ready()
    step(4)
    k_5()
    step(5)
    step(6)
    step(7)
    forward()
    att.start()
    att.across(0)
    step(8)
    att.across(1)
    step(9)
    att.ring(0)
    att.across(2)
    step(10)
    att.across(3)
    att.ring(1)
    backward()
    att.relay(0)
    att.ring(2)
    m_2()
    dq.across(1)
    att.relay(1)
    att.ring(3)
    dq.across(2)
    m_3()
    dq.across(3)
    dq.ring(0)
    att.relay(2)
    m_4()
    dq.ring(1)
    att.relay(3)
    dq.relay(0)
    m_5()
    dq.ring(2)
    dq.relay(1)
    tokens_t[...] = tall(tpan).T
    for n in range(4):
        att.done(n)
        output_part(n)
    output_send()
    dq.ring(3)
    dq.relay(2)
    w_output_grad(0)
    w_output_grad(1)
    kv_grad_part()
    dq.relay(3)
    w_output_grad(2)
    w_output_grad(3)
    output_end()
    for n in range(4):
        dq.done(n)
        token_grad_part(n)
        if n < 3:
            w_query_grad(n)
    t_part[...] = acc[...].astype(BF16).reshape(N, part_rows, -1)
    kept["t"] = fan("n", lambda i: t_part.at[i], lambda d: t_recv.at[d - 1], t_recv)
    w_query_grad(3)

    got(*kept["t"])
    sum_narrow(t_part, t_recv, t_out)
    store([(t_out, gtok_h)], t_out)
    for sem, ref in stores:
        local_done(sem, ref)
    for n in range(max(0, len(sends) - SEND_SEMS), len(sends)):
        wait_sent(n)


def last_kernel(*refs):
    loads = []
    for src, held, dst in zip(refs[:5], refs[10:15], refs[5:10]):
        n = PIECES if src.shape[0] * src.shape[1] > 2 ** 18 else 1
        size = src.shape[0] // n
        for i in range(n):
            at = slice(i * size, (i + 1) * size)
            c = pltpu.make_async_copy(src.at[at], held.at[at], refs[15].at[len(loads)])
            c.start()
            loads.append((c, held.at[at], dst.at[at]))
    stores = []
    for c, src, dst in loads:
        c.wait()
        stores.append(pltpu.make_async_copy(src, dst, refs[16].at[len(stores)]))
        stores[-1].start()
    for c in stores:
        c.wait()


def shards(K, N, tokens, w_query, w_keyval, w_output, grad_out):
    part_rows, feat = tokens.shape
    rows = part_rows * N
    R = rows // (K * K)
    qc = w_query.shape[1]
    Z = K
    C = 2 * Z
    U = qc // C
    B = K // 2
    assert w_keyval.shape[1] == 2 * HD and U % HD == 0 and N == 4 and K == 4

    def v(*shape):
        return pltpu.VMEM(shape, BF16)

    def reduce_buffers():
        return [
            v(2, 2, K, B, R, U), v(2, 2, K, B, R, U), v(2, 2, K, K, R, U), v(2, K, K, R, U),
            v(2, K - 1, K, R, U), v(2, K, R, U), v(K - 1, 2, R, U), v(2, R, U),
        ]

    def pair_buffers():
        return [
            v(2, K - 1, K, R, HD), v(2, K, R, HD), v(2, K - 1, R, HD), v(2, R, HD),
            v(2, K - 1, R, HD),
        ]

    def panel():
        return v(2, K, K, K, R, U)

    def pair_panel():
        return v(2, K, K, R, HD)

    scratch = (
        [v(C, feat, U), v(*w_keyval.shape), v(*w_output.shape)]
        + [v(N, part_rows, feat), v(N, part_rows, feat)]
        + [panel(), panel(), pair_panel(), pair_panel()]
        + reduce_buffers() + reduce_buffers() + pair_buffers() + pair_buffers()
        + [pair_panel(), pair_panel(), v(rows, 2 * HD), panel(), panel()]
        + [pltpu.VMEM((rows, feat), F32)]
        + [v(N, part_rows, feat), v(N - 1, part_rows, feat)] * 2
        + [v(part_rows, feat), v(part_rows, feat)]
        + [v(feat, rows), v(2, K, feat, U), v(*w_keyval.shape), v(2, K, U, feat)]
        + [pltpu.SemaphoreType.DMA((SEND_SEMS,)), pltpu.SemaphoreType.DMA((RECV_SEMS,))]
        + [pltpu.SemaphoreType.DMA((LOCAL_SEMS,))]
    )
    anywhere = pl.BlockSpec(memory_space=pl.ANY)

    def array(*shape):
        return jax.ShapeDtypeStruct(shape, BF16)

    shapes = (
        array(part_rows, feat), array(part_rows, feat),
        array(feat, qc), array(feat, 2 * HD), array(qc, feat),
    )
    results = pl.pallas_call(
        functools.partial(kernel, K, N),
        out_shape=shapes,
        in_specs=[anywhere] * 5,
        out_specs=(anywhere,) * 5,
        scratch_shapes=scratch,
        compiler_params=pltpu.CompilerParams(
            collective_id=0, has_side_effects=True, vmem_limit_bytes=56 * 1024 * 1024
        ),
        name="layer",
    )(tokens, w_query, w_keyval, w_output, grad_out)
    return pl.pallas_call(
        last_kernel,
        out_shape=shapes,
        in_specs=[anywhere] * 5,
        out_specs=(anywhere,) * 5,
        scratch_shapes=[v(*s.shape) for s in shapes]
        + [pltpu.SemaphoreType.DMA((3 + 2 * PIECES,))] * 2,
        compiler_params=pltpu.CompilerParams(vmem_limit_bytes=60 * 1024 * 1024),
        name="hand_over",
    )(*results)


def solution(mesh):
    N, wide = mesh.shape["narrow"], mesh.shape["wide"]
    K = next(k for k in range(1, wide + 1) if k ** 3 >= wide)
    assert K ** 3 == wide
    return jax.shard_map(
        functools.partial(shards, K, N),
        mesh=mesh,
        in_specs=(
            P("narrow", "wide"),
            P("wide", "narrow"),
            P("wide", "narrow"),
            P("narrow", "wide"),
            P("narrow", "wide"),
        ),
        out_specs=(
            P("narrow", "wide"),
            P("narrow", "wide"),
            P("wide", "narrow"),
            P("wide", "narrow"),
            P("narrow", "wide"),
        ),
        check_vma=False,
    )
```

```python
import functools

import jax
import jax.numpy as jnp
from jax import lax
from jax.experimental import pallas as pl
from jax.experimental.pallas import tpu as pltpu
from jax.sharding import PartitionSpec as P

HD = 128
F32 = jnp.float32
BF16 = jnp.bfloat16
MESH = pl.DeviceIdType.MESH
RECV_SEMS = 130
SEND_SEMS = 48
LOCAL_SEMS = 26
PIECES = 4
REDUCE_GROUPS = ((0, 1), (1, 2), (2, 3), (3, 4))
GATHER_GROUPS = ((0, 1), (1, 2), (2, 3), (3, 4))


def mm(left, right, dims):
    return lax.dot_general(left, right, (dims, ((), ())), preferred_element_type=F32)


NN = ((1,), (0,))
NT = ((1,), (1,))
TN = ((0,), (0,))


def kernel(
    K, N, tok, wq_h, wkv_h, wo_h, gout,
    out_h, gtok_h, gwq_h, gwkv_h, gwo_h,
    wq, wkv, wo, tpan, gpan, pq, pg, pkv, pkg,
    q_far, q_mid, q_near, qs1, q2, qs2, q3, qf,
    g_far, g_mid, g_near, gs1, g2, gs2, g3, gf,
    k1, ks1, k2, ks2, k3,
    m1, ms1, m2, ms2, m3,
    kvp, kgp, kg, ap, dp, acc, o_part, o_recv, t_part, t_recv, o_out, t_out,
    tokens_t, gwq_o, gwkv_o, gwo_o,
    send_sems, recv_sems, local_sems,
):
    Z = K
    B = K // 2
    R, U = pq.shape[4], pq.shape[5]
    rows = K * K * R
    C = 2 * Z
    me = lax.axis_index("wide")
    nar = lax.axis_index("narrow")
    z, x, y = me // (K * K), (me // K) % K, me % K
    part_rows = rows // N
    both = (0, 1)
    first = ("x", "y")
    second = ("y", "x")
    spot = (x, y)
    low, high = slice(0, B), slice(B, K)

    def peer(axis, d):
        if axis == "core":
            i = nar + 1 - 2 * (nar % 2)
            return {"narrow": i}, i
        if axis == "n":
            i = (nar + d) % N
            return {"narrow": i}, i
        if axis == "z":
            i = (z + d) % K
            return {"wide": i * K * K + x * K + y}, i
        if axis == "x":
            i = (x + d) % K
            return {"wide": z * K * K + i * K + y}, i
        i = (y + d) % K
        return {"wide": z * K * K + x * K + i}, i

    count = [0]
    sends = []

    def receiver():
        count[0] += 1
        return count[0] - 1

    def remote(axis, d, src, dst, send_sem, recv_sem):
        return pltpu.make_async_remote_copy(
            src_ref=src, dst_ref=dst, send_sem=send_sems.at[send_sem],
            recv_sem=recv_sems.at[recv_sem], device_id=peer(axis, d)[0], device_id_type=MESH,
        )

    def wait_sent(n):
        i, ref = sends[n]
        remote("core", 1, ref, ref, i, 0).wait_send()

    def batch(items, gone):
        n = len(sends)
        if n >= SEND_SEMS:
            wait_sent(n - SEND_SEMS)
        i = n % SEND_SEMS
        sends.append((i, gone))
        for axis, d, src, dst, r in items:
            remote(axis, d, src, dst, i, r).start()

    def got(r, ref):
        remote("core", 1, ref, ref, 0, r).wait_recv()

    def fan(axis, src, dst, whole):
        r = receiver()
        ds = range(1, N if axis == "n" else K)
        batch([(axis, d, src(peer(axis, d)[1]), dst(d), r) for d in ds], whole)
        return r, whole

    locals_used = [0]

    def local(pairs):
        sem = local_sems.at[locals_used[0]]
        locals_used[0] += 1
        for s, d in pairs:
            pltpu.make_async_copy(s, d, sem).start()
        return sem

    def local_done(sem, ref):
        pltpu.make_async_copy(ref, ref, sem).wait()

    tok_l = local([(tok, tpan.at[nar])])
    gout_l = local([(gout, gpan.at[nar])])
    wkv_l = local([(wkv_h, wkv)])
    wq_l = local([(wq_h.at[:, c * U:(c + 1) * U], wq.at[c]) for c in range(C)])
    wo_l = local([(wo_h, wo)])

    barrier = pltpu.get_barrier_semaphore()
    peers = [("n", d) for d in range(1, N)] + [(a, d) for a in "zxy" for d in range(1, K)]
    for a, d in peers:
        pl.semaphore_signal(barrier, inc=1, device_id=peer(a, d)[0], device_id_type=MESH)
    pl.semaphore_wait(barrier, len(peers))

    def share_start(own, pan):
        far, near = receiver(), receiver()
        batch(
            [("n", 2, own, pan.at[nar], far), ("core", 1, own, pan.at[nar], near)], pan.at[0:2]
        )
        return far, near

    def share_end(pan, far, near):
        other = (nar + 2) % N
        got(far, pan.at[0])
        batch([("core", 1, pan.at[other], pan.at[other], near)], pan.at[0])
        got(near, pan.at[0:2])

    tok_c = share_start(tok, tpan)
    gout_c = share_start(gout, gpan)

    def put(p, h, e, v):
        v = v.astype(BF16).reshape(K, K, R, -1)
        at = (h,) if e is None else (h, e)
        if h == 0:
            p[at] = v
        else:
            for i in range(K):
                p[at + (slice(0, K), i)] = v[i]

    def get(p, h, e):
        at = (h,) if e is None else (h, e)
        if h == 0:
            return p[at].reshape(rows, -1)
        return jnp.concatenate(
            [p[at + (slice(0, K), i)].reshape(K * R, -1) for i in range(K)], axis=0
        )

    def small1(p, recv):
        out = []
        for h in both:
            out.append(fan(first[h], lambda i: p.at[h, i], lambda d: recv.at[h, d - 1], recv.at[h]))
        return out

    def small2(waits, p, recv, s, recv2):
        out = []
        for h in both:
            got(*waits[h])
            total = p[h, spot[h]].astype(F32)
            for d in range(K - 1):
                total += recv[h, d].astype(F32)
            s[h] = total.astype(BF16)
            out.append(fan(second[h], lambda i: s.at[h, i], lambda d: recv2.at[h, d - 1], recv2.at[h]))
        return out

    def small3(waits, s, recv2, t, recv3):
        out = []
        for h in both:
            got(*waits[h])
            total = s[h, spot[1 - h]].astype(F32)
            for d in range(K - 1):
                total += recv2[h, d].astype(F32)
            t[h] = total.astype(BF16)
            out.append(fan("z", lambda i: t.at[h], lambda d: recv3.at[h, d - 1], recv3.at[h]))
        return out

    def small4(waits, t, recv3, p):
        out = []
        for h in both:
            got(*waits[h])
            total = t[h].astype(F32)
            for d in range(K - 1):
                total += recv3[h, d].astype(F32)
            p[h, spot[h], spot[1 - h]] = total.astype(BF16)
            here = p.at[h, spot[h], spot[1 - h]]
            out.append(fan(second[h], lambda i: here, lambda d: here, p.at[h, 0, 1:K]))
        return out

    def small5(waits, p):
        out = []
        for h in both:
            got(*waits[h])
            here = p.at[h, spot[h]]
            out.append(fan(first[h], lambda i: here, lambda d: here, p.at[h, 1:K]))
        return out

    def view(h, slots, i, part):
        return (h, slots, i, part)

    class Reduce:
        groups = REDUCE_GROUPS

        def __init__(self, p, far, mid, near, s1, r2, s2, r3, f):
            self.p, self.far, self.mid, self.near = p, far, mid, near
            self.s1, self.r2, self.s2, self.r3, self.f = s1, r2, s2, r3, f
            self.c1, self.c2 = {}, {}
            self.c3 = receiver()

        def weight(self, h, e):
            return h * Z + (z + 1 + e) % K

        def start(self, n):
            slots = slice(*self.groups[n])
            for h in both:
                i = spot[h]
                there, after, before = (i + 2) % K, (i + 1) % K, (i + K - 1) % K
                axis, p = first[h], self.p
                f, r = receiver(), receiver()
                self.c1[n, h] = f, r
                batch([
                    (axis, 1, p.at[view(h, slots, there, low)], self.far.at[h, 0, slots], f),
                    (axis, K - 1, p.at[view(h, slots, there, high)], self.far.at[h, 1, slots], f),
                    (axis, 1, p.at[view(h, slots, after, high)], self.near.at[h, 0, slots, high], r),
                    (axis, K - 1, p.at[view(h, slots, before, low)], self.near.at[h, 1, slots, low], r),
                ], self.near.at[h, :, slots])

        def relay(self, n):
            slots = slice(*self.groups[n])
            for h in both:
                i = spot[h]
                f, r = self.c1[n, h]
                got(f, self.far.at[h, :, slots])
                items = []
                for side, d, part in ((0, 1, low), (1, K - 1, high)):
                    for e in range(*self.groups[n]):
                        own = self.p[view(h, e, (i + d) % K, part)].astype(F32)
                        total = own + self.far[h, side, e].astype(F32)
                        self.mid[h, side, e] = total.astype(BF16)
                    items.append((
                        first[h], d, self.mid.at[h, side, slots],
                        self.near.at[h, side, slots, part], r,
                    ))
                batch(items, self.mid.at[h, :, slots])

        def collect(self, n):
            slots = slice(*self.groups[n])
            for h in both:
                got(self.c1[n, h][1], self.near.at[h, :, slots])
                for e in range(*self.groups[n]):
                    total = self.p[view(h, e, spot[h], slice(0, K))].astype(F32)
                    total += self.near[h, 0, e].astype(F32)
                    total += self.near[h, 1, e].astype(F32)
                    self.s1[h, e] = total.astype(BF16)
                self.c2[n, h] = fan(
                    second[h], lambda i: self.s1.at[h, slots, i],
                    lambda d: self.r2.at[h, d - 1, slots], self.r2.at[h, :, slots],
                )

        def across(self, n):
            for h in both:
                got(*self.c2[n, h])
                for e in range(*self.groups[n]):
                    total = self.s1[h, e, spot[1 - h]].astype(F32)
                    for d in range(K - 1):
                        total += self.r2[h, d, e].astype(F32)
                    self.s2[h, e] = total.astype(BF16)
            items = [
                ("z", e + 1, self.s2.at[:, e], self.r3.at[e], self.c3)
                for e in range(*self.groups[n]) if e < K - 1
            ]
            if items:
                batch(items, self.r3.at[0:len(items)])

        def finish(self):
            got(self.c3, self.r3)
            total = self.s2[:, K - 1].astype(F32)
            for d in range(K - 1):
                total += self.r3[d].astype(F32)
            self.f[...] = total.astype(BF16)

    class Gather:
        groups = GATHER_GROUPS

        def __init__(self, p):
            self.p = p
            self.c1, self.c2, self.c3, self.c4 = [], {}, {}, {}

        def weight(self, h, e):
            return h * Z + (z + K - e) % K

        def start(self):
            p = self.p
            self.c1 = [receiver() for d in range(1, K)]
            batch(
                [
                    ("z", d, p.at[h, 0, spot[h], spot[1 - h]], p.at[h, d, spot[h], spot[1 - h]],
                     self.c1[d - 1])
                    for d in range(1, K) for h in both
                ],
                p.at[:, 1:K, 0, 0],
            )

        def across(self, n):
            e0, e1 = self.groups[n]
            for e in range(max(e0, 1), e1):
                got(self.c1[e - 1], self.p.at[:, e, 0, 0])
            for h in both:
                here = self.p.at[h, e0:e1, spot[h], spot[1 - h]]
                self.c2[n, h] = fan(
                    second[h], lambda i: here, lambda d: here, self.p.at[h, e0:e1, 0, 1:K]
                )

        def ring(self, n):
            slots = slice(*self.groups[n])
            for h in both:
                got(*self.c2[n, h])
                here = self.p.at[view(h, slots, spot[h], slice(0, K))]
                r = receiver()
                self.c3[n, h] = r
                batch([(first[h], d, here, here, r) for d in (1, K - 1)], self.p.at[h, slots, 0:2])

        def relay(self, n):
            slots = slice(*self.groups[n])
            for h in both:
                got(self.c3[n, h], self.p.at[h, slots, 0:2])
                r = receiver()
                self.c4[n, h] = r
                items = []
                for d, part in ((1, low), (K - 1, high)):
                    here = self.p.at[view(h, slots, (spot[h] + K - d) % K, part)]
                    items.append((first[h], d, here, here, r))
                batch(items, self.p.at[h, slots, 0])

        def done(self, n):
            slots = slice(*self.groups[n])
            for h in both:
                got(self.c4[n, h], self.p.at[h, slots, 0])

    def tall(pan):
        return pan[...].reshape(rows, -1)

    local_done(tok_l, tok)
    share_end(tpan, *tok_c)
    local_done(wkv_l, wkv)
    kv = mm(tall(tpan), wkv[...], NN).astype(BF16)
    for h in both:
        put(pkv, h, None, kv[:, h * HD:(h + 1) * HD])
    k_c = small1(pkv, k1)
    local_done(wq_l, wq)

    q = Reduce(pq, q_far, q_mid, q_near, qs1, q2, qs2, q3, qf)
    g = Reduce(pg, g_far, g_mid, g_near, gs1, g2, gs2, g3, gf)

    def project(n):
        for e in range(*q.groups[n]):
            for h in both:
                put(pq, h, e, mm(tall(tpan), wq[q.weight(h, e)], NN))

    def back_out(n):
        for e in range(*g.groups[n]):
            for h in both:
                at = pl.multiple_of(g.weight(h, e) * U, U)
                put(pg, h, e, mm(tall(gpan), wo[pl.ds(at, U), :], NT))

    G = len(REDUCE_GROUPS)
    work = [(q, n) for n in range(G)] + [(g, n) for n in range(G)]

    def compute(t):
        s, n = work[t]
        (project if s is q else back_out)(n)

    def start(t):
        work[t][0].start(work[t][1])

    def relay(t):
        work[t][0].relay(work[t][1])

    def collect(t):
        work[t][0].collect(work[t][1])

    def across(t):
        work[t][0].across(work[t][1])

    def g_ready():
        share_end(gpan, *gout_c)
        local_done(gout_l, gout)
        local_done(wo_l, wo)

    def heads(f):
        return jnp.concatenate(
            [f[h, :, k * HD:(k + 1) * HD] for h in both for k in range(U // HD)], axis=0
        )

    def unheads(p, v):
        per = U // HD
        for h in both:
            p[h, 0, spot[h], spot[1 - h]] = jnp.concatenate(
                [v[(h * per + k) * R:(h * per + k + 1) * R] for k in range(per)], axis=1
            )

    scale = HD ** (-0.5)
    kept = {}

    def output_end():
        got(*kept["o"])
        sum_narrow(o_part, o_recv, o_out)
        store([(o_out, out_h)], o_out)

    def forward():
        q.finish()
        for h in both:
            got(*kept["k"][h])
        queries = heads(qf)
        keys = get(kvp, 0, None)
        values = get(kvp, 1, None)
        scores = mm(queries, keys, NT) * scale
        place = lax.broadcasted_iota(jnp.int32, scores.shape, 0) % R + (x * K + y) * R
        allowed = lax.broadcasted_iota(jnp.int32, scores.shape, 1) <= place
        weights = jnp.where(allowed, jnp.exp(scores), 0.0)
        weights = weights / jnp.sum(weights, axis=1, keepdims=True)
        probs = weights.astype(BF16)
        unheads(ap, mm(probs, values, NN).astype(BF16))
        kept["fwd"] = queries, keys, values, weights, probs

    def backward():
        g.finish()
        queries, keys, values, weights, probs = kept["fwd"]
        cotangent = heads(gf)
        prob_grad = mm(cotangent, values, NT)
        score_grad = weights * (prob_grad - jnp.sum(weights * prob_grad, axis=1, keepdims=True))
        score_half = score_grad.astype(BF16)
        unheads(dp, (mm(score_half, keys, NN) * scale).astype(BF16))
        dq.start()
        dq.across(0)
        grad_keys = mm(score_half, queries, TN) * scale
        grad_values = mm(probs, cotangent, TN)
        put(pkg, 0, None, grad_keys)
        put(pkg, 1, None, grad_values)
        kept["m"] = small1(pkg, m1)

    att = Gather(ap)
    dq = Gather(dp)
    stores = []

    def store(pairs, ref):
        stores.append((local(pairs), ref))

    def sum_narrow(part, recv, o):
        total = part[nar].astype(F32)
        for d in range(N - 1):
            total += recv[d].astype(F32)
        o[...] = total.astype(BF16)

    def w_output_grad(n):
        for e in range(*att.groups[n]):
            for h in both:
                c = att.weight(h, e)
                gwo_o[h, e] = mm(get(ap, h, e), tall(gpan), TN).astype(BF16)
                store([(gwo_o.at[h, e], gwo_h.at[pl.ds(pl.multiple_of(c * U, U), U), :])], gwo_o.at[h, e])

    def w_query_grad(n):
        for e in range(*dq.groups[n]):
            for h in both:
                c = dq.weight(h, e)
                gwq_o[h, e] = mm(tokens_t[...], get(dp, h, e), NN).astype(BF16)
                store([(gwq_o.at[h, e], gwq_h.at[:, pl.ds(pl.multiple_of(c * U, U), U)])], gwq_o.at[h, e])

    def add(term, start=False):
        acc[...] = term if start else acc[...] + term

    def output_part(n):
        for e in range(*att.groups[n]):
            for h in both:
                at = pl.multiple_of(att.weight(h, e) * U, U)
                add(mm(get(ap, h, e), wo[pl.ds(at, U), :], NN), e == 0 and h == 0)

    def output_send():
        o_part[...] = acc[...].astype(BF16).reshape(N, part_rows, -1)
        kept["o"] = fan("n", lambda i: o_part.at[i], lambda d: o_recv.at[d - 1], o_recv)

    def kv_grad_part():
        for h in both:
            got(*kept["m"][h])
        kg[...] = jnp.concatenate([get(kgp, h, None) for h in both], axis=1)
        gwkv_o[...] = mm(tokens_t[...], kg[...], NN).astype(BF16)
        store([(gwkv_o, gwkv_h)], gwkv_o)
        add(mm(kg[...], wkv[...], NT), True)

    def token_grad_part(n):
        for e in range(*dq.groups[n]):
            for h in both:
                add(mm(get(dp, h, e), wq[dq.weight(h, e)], NT))

    def m_2():
        kept["m"] = small2(kept["m"], pkg, m1, ms1, m2)

    def m_3():
        kept["m"] = small3(kept["m"], ms1, m2, ms2, m3)

    def m_4():
        kept["m"] = small4(kept["m"], ms2, m3, kgp)

    def m_5():
        kept["m"] = small5(kept["m"], kgp)

    def k_2():
        kept["k"] = small2(k_c, pkv, k1, ks1, k2)

    def k_3():
        kept["k"] = small3(kept["k"], ks1, k2, ks2, k3)

    def k_4():
        kept["k"] = small4(kept["k"], ks2, k3, kvp)

    def k_5():
        kept["k"] = small5(kept["k"], kvp)

    compute(0)
    start(0)
    compute(1)
    start(1)
    compute(2)
    start(2)
    relay(0)
    k_2()
    compute(3)
    start(3)
    relay(1)
    collect(0)
    k_3()
    g_ready()
    compute(4)
    start(4)
    relay(2)
    collect(1)
    across(0)
    k_4()
    compute(5)
    start(5)
    relay(3)
    collect(2)
    across(1)
    k_5()
    compute(6)
    start(6)
    relay(4)
    collect(3)
    across(2)
    compute(7)
    start(7)
    relay(5)
    collect(4)
    across(3)
    relay(6)
    collect(5)
    across(4)
    forward()
    att.start()
    att.across(0)
    relay(7)
    collect(6)
    across(5)
    att.across(1)
    collect(7)
    across(6)
    att.ring(0)
    att.across(2)
    across(7)
    att.across(3)
    att.ring(1)
    backward()
    att.ring(2)
    att.relay(0)
    att.ring(3)
    m_2()
    att.relay(1)
    dq.across(1)
    dq.across(2)
    dq.ring(0)
    m_3()
    dq.across(3)
    dq.ring(1)
    att.relay(2)
    m_4()
    dq.ring(2)
    att.relay(3)
    dq.relay(0)
    dq.ring(3)
    m_5()
    dq.relay(1)
    att.done(0)
    output_part(0)
    att.done(1)
    output_part(1)
    dq.relay(2)
    att.done(2)
    output_part(2)
    att.done(3)
    output_part(3)
    dq.relay(3)
    output_send()
    tokens_t[...] = tall(tpan).T
    kv_grad_part()
    dq.done(0)
    token_grad_part(0)
    dq.done(1)
    token_grad_part(1)
    dq.done(2)
    token_grad_part(2)
    dq.done(3)
    token_grad_part(3)
    t_part[...] = acc[...].astype(BF16).reshape(N, part_rows, -1)
    kept["t"] = fan("n", lambda i: t_part.at[i], lambda d: t_recv.at[d - 1], t_recv)
    w_output_grad(0)
    w_output_grad(1)
    w_output_grad(2)
    w_output_grad(3)
    output_end()
    w_query_grad(0)
    w_query_grad(1)
    w_query_grad(2)
    w_query_grad(3)

    got(*kept["t"])
    sum_narrow(t_part, t_recv, t_out)
    store([(t_out, gtok_h)], t_out)
    for sem, ref in stores:
        local_done(sem, ref)
    for n in range(max(0, len(sends) - SEND_SEMS), len(sends)):
        wait_sent(n)


def last_kernel(*refs):
    loads = []
    for src, held, dst in zip(refs[:5], refs[10:15], refs[5:10]):
        n = PIECES if src.shape[0] * src.shape[1] > 2 ** 18 else 1
        size = src.shape[0] // n
        for i in range(n):
            at = slice(i * size, (i + 1) * size)
            c = pltpu.make_async_copy(src.at[at], held.at[at], refs[15].at[len(loads)])
            c.start()
            loads.append((c, held.at[at], dst.at[at]))
    stores = []
    for c, src, dst in loads:
        c.wait()
        stores.append(pltpu.make_async_copy(src, dst, refs[16].at[len(stores)]))
        stores[-1].start()
    for c in stores:
        c.wait()


def shards(K, N, tokens, w_query, w_keyval, w_output, grad_out):
    part_rows, feat = tokens.shape
    rows = part_rows * N
    R = rows // (K * K)
    qc = w_query.shape[1]
    Z = K
    C = 2 * Z
    U = qc // C
    B = K // 2
    assert w_keyval.shape[1] == 2 * HD and U % HD == 0 and N == 4 and K == 4

    def v(*shape):
        return pltpu.VMEM(shape, BF16)

    def reduce_buffers():
        return [
            v(2, 2, K, B, R, U), v(2, 2, K, B, R, U), v(2, 2, K, K, R, U), v(2, K, K, R, U),
            v(2, K - 1, K, R, U), v(2, K, R, U), v(K - 1, 2, R, U), v(2, R, U),
        ]

    def pair_buffers():
        return [
            v(2, K - 1, K, R, HD), v(2, K, R, HD), v(2, K - 1, R, HD), v(2, R, HD),
            v(2, K - 1, R, HD),
        ]

    def panel():
        return v(2, K, K, K, R, U)

    def pair_panel():
        return v(2, K, K, R, HD)

    scratch = (
        [v(C, feat, U), v(*w_keyval.shape), v(*w_output.shape)]
        + [v(N, part_rows, feat), v(N, part_rows, feat)]
        + [panel(), panel(), pair_panel(), pair_panel()]
        + reduce_buffers() + reduce_buffers() + pair_buffers() + pair_buffers()
        + [pair_panel(), pair_panel(), v(rows, 2 * HD), panel(), panel()]
        + [pltpu.VMEM((rows, feat), F32)]
        + [v(N, part_rows, feat), v(N - 1, part_rows, feat)] * 2
        + [v(part_rows, feat), v(part_rows, feat)]
        + [v(feat, rows), v(2, K, feat, U), v(*w_keyval.shape), v(2, K, U, feat)]
        + [pltpu.SemaphoreType.DMA((SEND_SEMS,)), pltpu.SemaphoreType.DMA((RECV_SEMS,))]
        + [pltpu.SemaphoreType.DMA((LOCAL_SEMS,))]
    )
    anywhere = pl.BlockSpec(memory_space=pl.ANY)

    def array(*shape):
        return jax.ShapeDtypeStruct(shape, BF16)

    shapes = (
        array(part_rows, feat), array(part_rows, feat),
        array(feat, qc), array(feat, 2 * HD), array(qc, feat),
    )
    results = pl.pallas_call(
        functools.partial(kernel, K, N),
        out_shape=shapes,
        in_specs=[anywhere] * 5,
        out_specs=(anywhere,) * 5,
        scratch_shapes=scratch,
        compiler_params=pltpu.CompilerParams(
            collective_id=0, has_side_effects=True, vmem_limit_bytes=56 * 1024 * 1024
        ),
        name="layer",
    )(tokens, w_query, w_keyval, w_output, grad_out)
    return pl.pallas_call(
        last_kernel,
        out_shape=shapes,
        in_specs=[anywhere] * 5,
        out_specs=(anywhere,) * 5,
        scratch_shapes=[v(*s.shape) for s in shapes]
        + [pltpu.SemaphoreType.DMA((3 + 2 * PIECES,))] * 2,
        compiler_params=pltpu.CompilerParams(vmem_limit_bytes=60 * 1024 * 1024),
        name="hand_over",
    )(*results)


def solution(mesh):
    N, wide = mesh.shape["narrow"], mesh.shape["wide"]
    K = next(k for k in range(1, wide + 1) if k ** 3 >= wide)
    assert K ** 3 == wide
    return jax.shard_map(
        functools.partial(shards, K, N),
        mesh=mesh,
        in_specs=(
            P("narrow", "wide"),
            P("wide", "narrow"),
            P("wide", "narrow"),
            P("narrow", "wide"),
            P("narrow", "wide"),
        ),
        out_specs=(
            P("narrow", "wide"),
            P("narrow", "wide"),
            P("wide", "narrow"),
            P("wide", "narrow"),
            P("narrow", "wide"),
        ),
        check_vma=False,
    )
```

```python
import functools

import jax
import jax.numpy as jnp
from jax import lax
from jax.experimental import pallas as pl
from jax.experimental.pallas import tpu as pltpu
from jax.sharding import PartitionSpec as P

HD = 128
F32 = jnp.float32
BF16 = jnp.bfloat16
MESH = pl.DeviceIdType.MESH
RECV_SEMS = 130
SEND_SEMS = 48
LOCAL_SEMS = 26
PIECES = 4
REDUCE_GROUPS = ((0, 1), (1, 2), (2, 3), (3, 4))
GATHER_GROUPS = ((0, 1), (1, 2), (2, 3), (3, 4))


def mm(left, right, dims):
    return lax.dot_general(left, right, (dims, ((), ())), preferred_element_type=F32)


NN = ((1,), (0,))
NT = ((1,), (1,))
TN = ((0,), (0,))


def kernel(
    K, N, tok, wq_h, wkv_h, wo_h, gout,
    out_h, gtok_h, gwq_h, gwkv_h, gwo_h,
    wq, wkv, wo, tpan, gpan, pq, pg, pkv, pkg,
    q_far, q_mid, q_near, qs1, q2, qs2, q3, qf,
    g_far, g_mid, g_near, gs1, g2, gs2, g3, gf,
    k1, ks1, k2, ks2, k3,
    m1, ms1, m2, ms2, m3,
    kvp, kgp, kg, ap, dp, acc, o_part, o_recv, t_part, t_recv, o_out, t_out,
    tokens_t, gwq_o, gwkv_o, gwo_o,
    send_sems, recv_sems, local_sems,
):
    Z = K
    B = K // 2
    R, U = pq.shape[4], pq.shape[5]
    rows = K * K * R
    C = 2 * Z
    me = lax.axis_index("wide")
    nar = lax.axis_index("narrow")
    z, x, y = me // (K * K), (me // K) % K, me % K
    part_rows = rows // N
    both = (0, 1)
    first = ("x", "y")
    second = ("y", "x")
    spot = (x, y)
    low, high = slice(0, B), slice(B, K)

    def peer(axis, d):
        if axis == "core":
            i = nar + 1 - 2 * (nar % 2)
            return {"narrow": i}, i
        if axis == "n":
            i = (nar + d) % N
            return {"narrow": i}, i
        if axis == "z":
            i = (z + d) % K
            return {"wide": i * K * K + x * K + y}, i
        if axis == "x":
            i = (x + d) % K
            return {"wide": z * K * K + i * K + y}, i
        i = (y + d) % K
        return {"wide": z * K * K + x * K + i}, i

    count = [0]
    sends = []

    def receiver():
        count[0] += 1
        return count[0] - 1

    def remote(axis, d, src, dst, send_sem, recv_sem):
        return pltpu.make_async_remote_copy(
            src_ref=src, dst_ref=dst, send_sem=send_sems.at[send_sem],
            recv_sem=recv_sems.at[recv_sem], device_id=peer(axis, d)[0], device_id_type=MESH,
        )

    def wait_sent(n):
        i, ref = sends[n]
        remote("core", 1, ref, ref, i, 0).wait_send()

    def batch(items, gone):
        n = len(sends)
        if n >= SEND_SEMS:
            wait_sent(n - SEND_SEMS)
        i = n % SEND_SEMS
        sends.append((i, gone))
        for axis, d, src, dst, r in items:
            remote(axis, d, src, dst, i, r).start()

    def got(r, ref):
        remote("core", 1, ref, ref, 0, r).wait_recv()

    def fan(axis, src, dst, whole):
        r = receiver()
        ds = range(1, N if axis == "n" else K)
        batch([(axis, d, src(peer(axis, d)[1]), dst(d), r) for d in ds], whole)
        return r, whole

    locals_used = [0]

    def local(pairs):
        sem = local_sems.at[locals_used[0]]
        locals_used[0] += 1
        for s, d in pairs:
            pltpu.make_async_copy(s, d, sem).start()
        return sem

    def local_done(sem, ref):
        pltpu.make_async_copy(ref, ref, sem).wait()

    tok_l = local([(tok, tpan.at[nar])])
    gout_l = local([(gout, gpan.at[nar])])
    wkv_l = local([(wkv_h, wkv)])
    wq_l = local([(wq_h.at[:, c * U:(c + 1) * U], wq.at[c]) for c in range(C)])
    wo_l = local([(wo_h, wo)])

    barrier = pltpu.get_barrier_semaphore()
    peers = [("n", d) for d in range(1, N)] + [(a, d) for a in "zxy" for d in range(1, K)]
    for a, d in peers:
        pl.semaphore_signal(barrier, inc=1, device_id=peer(a, d)[0], device_id_type=MESH)
    pl.semaphore_wait(barrier, len(peers))

    def share_start(own, pan):
        far, near = receiver(), receiver()
        batch(
            [("n", 2, own, pan.at[nar], far), ("core", 1, own, pan.at[nar], near)], pan.at[0:2]
        )
        return far, near

    def share_end(pan, far, near):
        other = (nar + 2) % N
        got(far, pan.at[0])
        batch([("core", 1, pan.at[other], pan.at[other], near)], pan.at[0])
        got(near, pan.at[0:2])

    tok_c = share_start(tok, tpan)
    gout_c = share_start(gout, gpan)

    def put(p, h, e, v):
        v = v.astype(BF16).reshape(K, K, R, -1)
        at = (h,) if e is None else (h, e)
        if h == 0:
            p[at] = v
        else:
            for i in range(K):
                p[at + (slice(0, K), i)] = v[i]

    def get(p, h, e):
        at = (h,) if e is None else (h, e)
        if h == 0:
            return p[at].reshape(rows, -1)
        return jnp.concatenate(
            [p[at + (slice(0, K), i)].reshape(K * R, -1) for i in range(K)], axis=0
        )

    def small1(p, recv):
        out = []
        for h in both:
            out.append(fan(first[h], lambda i: p.at[h, i], lambda d: recv.at[h, d - 1], recv.at[h]))
        return out

    def small2(waits, p, recv, s, recv2):
        out = []
        for h in both:
            got(*waits[h])
            total = p[h, spot[h]].astype(F32)
            for d in range(K - 1):
                total += recv[h, d].astype(F32)
            s[h] = total.astype(BF16)
            out.append(fan(second[h], lambda i: s.at[h, i], lambda d: recv2.at[h, d - 1], recv2.at[h]))
        return out

    def small3(waits, s, recv2, t, recv3):
        out = []
        for h in both:
            got(*waits[h])
            total = s[h, spot[1 - h]].astype(F32)
            for d in range(K - 1):
                total += recv2[h, d].astype(F32)
            t[h] = total.astype(BF16)
            out.append(fan("z", lambda i: t.at[h], lambda d: recv3.at[h, d - 1], recv3.at[h]))
        return out

    def small4(waits, t, recv3, p):
        out = []
        for h in both:
            got(*waits[h])
            total = t[h].astype(F32)
            for d in range(K - 1):
                total += recv3[h, d].astype(F32)
            p[h, spot[h], spot[1 - h]] = total.astype(BF16)
            here = p.at[h, spot[h], spot[1 - h]]
            out.append(fan(second[h], lambda i: here, lambda d: here, p.at[h, 0, 1:K]))
        return out

    def small5(waits, p):
        out = []
        for h in both:
            got(*waits[h])
            here = p.at[h, spot[h]]
            out.append(fan(first[h], lambda i: here, lambda d: here, p.at[h, 1:K]))
        return out

    def view(h, slots, i, part):
        return (h, slots, i, part)

    class Reduce:
        groups = REDUCE_GROUPS

        def __init__(self, p, far, mid, near, s1, r2, s2, r3, f):
            self.p, self.far, self.mid, self.near = p, far, mid, near
            self.s1, self.r2, self.s2, self.r3, self.f = s1, r2, s2, r3, f
            self.c1, self.c2 = {}, {}
            self.c3 = receiver()

        def weight(self, h, e):
            return h * Z + (z + 1 + e) % K

        def start(self, n):
            slots = slice(*self.groups[n])
            for h in both:
                i = spot[h]
                there, after, before = (i + 2) % K, (i + 1) % K, (i + K - 1) % K
                axis, p = first[h], self.p
                f, r = receiver(), receiver()
                self.c1[n, h] = f, r
                batch([
                    (axis, 1, p.at[view(h, slots, there, low)], self.far.at[h, 0, slots], f),
                    (axis, K - 1, p.at[view(h, slots, there, high)], self.far.at[h, 1, slots], f),
                    (axis, 1, p.at[view(h, slots, after, high)], self.near.at[h, 0, slots, high], r),
                    (axis, K - 1, p.at[view(h, slots, before, low)], self.near.at[h, 1, slots, low], r),
                ], self.near.at[h, :, slots])

        def relay(self, n):
            slots = slice(*self.groups[n])
            for h in both:
                i = spot[h]
                f, r = self.c1[n, h]
                got(f, self.far.at[h, :, slots])
                items = []
                for side, d, part in ((0, 1, low), (1, K - 1, high)):
                    for e in range(*self.groups[n]):
                        own = self.p[view(h, e, (i + d) % K, part)].astype(F32)
                        total = own + self.far[h, side, e].astype(F32)
                        self.mid[h, side, e] = total.astype(BF16)
                    items.append((
                        first[h], d, self.mid.at[h, side, slots],
                        self.near.at[h, side, slots, part], r,
                    ))
                batch(items, self.mid.at[h, :, slots])

        def collect(self, n):
            slots = slice(*self.groups[n])
            for h in both:
                got(self.c1[n, h][1], self.near.at[h, :, slots])
                for e in range(*self.groups[n]):
                    total = self.p[view(h, e, spot[h], slice(0, K))].astype(F32)
                    total += self.near[h, 0, e].astype(F32)
                    total += self.near[h, 1, e].astype(F32)
                    self.s1[h, e] = total.astype(BF16)
                self.c2[n, h] = fan(
                    second[h], lambda i: self.s1.at[h, slots, i],
                    lambda d: self.r2.at[h, d - 1, slots], self.r2.at[h, :, slots],
                )

        def across(self, n):
            for h in both:
                got(*self.c2[n, h])
                for e in range(*self.groups[n]):
                    total = self.s1[h, e, spot[1 - h]].astype(F32)
                    for d in range(K - 1):
                        total += self.r2[h, d, e].astype(F32)
                    self.s2[h, e] = total.astype(BF16)
            items = [
                ("z", e + 1, self.s2.at[:, e], self.r3.at[e], self.c3)
                for e in range(*self.groups[n]) if e < K - 1
            ]
            if items:
                batch(items, self.r3.at[0:len(items)])

        def finish(self):
            got(self.c3, self.r3)
            total = self.s2[:, K - 1].astype(F32)
            for d in range(K - 1):
                total += self.r3[d].astype(F32)
            self.f[...] = total.astype(BF16)

    class Gather:
        groups = GATHER_GROUPS

        def __init__(self, p):
            self.p = p
            self.c1, self.c2, self.c3, self.c4 = [], {}, {}, {}

        def weight(self, h, e):
            return h * Z + (z + K - e) % K

        def start(self):
            p = self.p
            self.c1 = [receiver() for d in range(1, K)]
            batch(
                [
                    ("z", d, p.at[h, 0, spot[h], spot[1 - h]], p.at[h, d, spot[h], spot[1 - h]],
                     self.c1[d - 1])
                    for d in range(1, K) for h in both
                ],
                p.at[:, 1:K, 0, 0],
            )

        def across(self, n):
            e0, e1 = self.groups[n]
            for e in range(max(e0, 1), e1):
                got(self.c1[e - 1], self.p.at[:, e, 0, 0])
            for h in both:
                here = self.p.at[h, e0:e1, spot[h], spot[1 - h]]
                self.c2[n, h] = fan(
                    second[h], lambda i: here, lambda d: here, self.p.at[h, e0:e1, 0, 1:K]
                )

        def ring(self, n):
            slots = slice(*self.groups[n])
            for h in both:
                got(*self.c2[n, h])
                here = self.p.at[view(h, slots, spot[h], slice(0, K))]
                r = receiver()
                self.c3[n, h] = r
                batch([(first[h], d, here, here, r) for d in (1, K - 1)], self.p.at[h, slots, 0:2])

        def relay(self, n):
            slots = slice(*self.groups[n])
            for h in both:
                got(self.c3[n, h], self.p.at[h, slots, 0:2])
                r = receiver()
                self.c4[n, h] = r
                items = []
                for d, part in ((1, low), (K - 1, high)):
                    here = self.p.at[view(h, slots, (spot[h] + K - d) % K, part)]
                    items.append((first[h], d, here, here, r))
                batch(items, self.p.at[h, slots, 0])

        def done(self, n):
            slots = slice(*self.groups[n])
            for h in both:
                got(self.c4[n, h], self.p.at[h, slots, 0])

    def tall(pan):
        return pan[...].reshape(rows, -1)

    local_done(tok_l, tok)
    share_end(tpan, *tok_c)
    local_done(wq_l, wq)

    q = Reduce(pq, q_far, q_mid, q_near, qs1, q2, qs2, q3, qf)
    g = Reduce(pg, g_far, g_mid, g_near, gs1, g2, gs2, g3, gf)

    def project(n):
        for e in range(*q.groups[n]):
            for h in both:
                put(pq, h, e, mm(tall(tpan), wq[q.weight(h, e)], NN))

    def back_out(n):
        for e in range(*g.groups[n]):
            for h in both:
                at = pl.multiple_of(g.weight(h, e) * U, U)
                put(pg, h, e, mm(tall(gpan), wo[pl.ds(at, U), :], NT))

    G = len(REDUCE_GROUPS)
    work = [(q, n) for n in range(G)] + [(g, n) for n in range(G)]

    def compute(t):
        s, n = work[t]
        (project if s is q else back_out)(n)

    def start(t):
        work[t][0].start(work[t][1])

    def relay(t):
        work[t][0].relay(work[t][1])

    def collect(t):
        work[t][0].collect(work[t][1])

    def across(t):
        work[t][0].across(work[t][1])

    def g_ready():
        share_end(gpan, *gout_c)
        local_done(gout_l, gout)
        local_done(wo_l, wo)

    def heads(f):
        return jnp.concatenate(
            [f[h, :, k * HD:(k + 1) * HD] for h in both for k in range(U // HD)], axis=0
        )

    def unheads(p, v):
        per = U // HD
        for h in both:
            p[h, 0, spot[h], spot[1 - h]] = jnp.concatenate(
                [v[(h * per + k) * R:(h * per + k + 1) * R] for k in range(per)], axis=1
            )

    scale = HD ** (-0.5)
    kept = {}

    def output_end():
        got(*kept["o"])
        sum_narrow(o_part, o_recv, o_out)
        store([(o_out, out_h)], o_out)

    def forward():
        q.finish()
        for h in both:
            got(*kept["k"][h])
        queries = heads(qf)
        keys = get(kvp, 0, None)
        values = get(kvp, 1, None)
        scores = mm(queries, keys, NT) * scale
        place = lax.broadcasted_iota(jnp.int32, scores.shape, 0) % R + (x * K + y) * R
        allowed = lax.broadcasted_iota(jnp.int32, scores.shape, 1) <= place
        weights = jnp.where(allowed, jnp.exp(scores), 0.0)
        weights = weights / jnp.sum(weights, axis=1, keepdims=True)
        probs = weights.astype(BF16)
        unheads(ap, mm(probs, values, NN).astype(BF16))
        kept["fwd"] = queries, keys, values, weights, probs

    def backward():
        g.finish()
        queries, keys, values, weights, probs = kept["fwd"]
        cotangent = heads(gf)
        prob_grad = mm(cotangent, values, NT)
        score_grad = weights * (prob_grad - jnp.sum(weights * prob_grad, axis=1, keepdims=True))
        score_half = score_grad.astype(BF16)
        unheads(dp, (mm(score_half, keys, NN) * scale).astype(BF16))
        dq.start()
        dq.across(0)
        grad_keys = mm(score_half, queries, TN) * scale
        grad_values = mm(probs, cotangent, TN)
        put(pkg, 0, None, grad_keys)
        put(pkg, 1, None, grad_values)
        kept["m"] = small1(pkg, m1)

    att = Gather(ap)
    dq = Gather(dp)
    stores = []

    def store(pairs, ref):
        stores.append((local(pairs), ref))

    def sum_narrow(part, recv, o):
        total = part[nar].astype(F32)
        for d in range(N - 1):
            total += recv[d].astype(F32)
        o[...] = total.astype(BF16)

    def w_output_grad(n):
        for e in range(*att.groups[n]):
            for h in both:
                c = att.weight(h, e)
                gwo_o[h, e] = mm(get(ap, h, e), tall(gpan), TN).astype(BF16)
                store([(gwo_o.at[h, e], gwo_h.at[pl.ds(pl.multiple_of(c * U, U), U), :])], gwo_o.at[h, e])

    def w_query_grad(n):
        for e in range(*dq.groups[n]):
            for h in both:
                c = dq.weight(h, e)
                gwq_o[h, e] = mm(tokens_t[...], get(dp, h, e), NN).astype(BF16)
                store([(gwq_o.at[h, e], gwq_h.at[:, pl.ds(pl.multiple_of(c * U, U), U)])], gwq_o.at[h, e])

    def add(term, start=False):
        acc[...] = term if start else acc[...] + term

    def output_part(n):
        for e in range(*att.groups[n]):
            for h in both:
                at = pl.multiple_of(att.weight(h, e) * U, U)
                add(mm(get(ap, h, e), wo[pl.ds(at, U), :], NN), e == 0 and h == 0)

    def output_send():
        o_part[...] = acc[...].astype(BF16).reshape(N, part_rows, -1)
        kept["o"] = fan("n", lambda i: o_part.at[i], lambda d: o_recv.at[d - 1], o_recv)

    def kv_grad_part():
        for h in both:
            got(*kept["m"][h])
        kg[...] = jnp.concatenate([get(kgp, h, None) for h in both], axis=1)
        gwkv_o[...] = mm(tokens_t[...], kg[...], NN).astype(BF16)
        store([(gwkv_o, gwkv_h)], gwkv_o)
        add(mm(kg[...], wkv[...], NT), True)

    def token_grad_part(n):
        for e in range(*dq.groups[n]):
            for h in both:
                add(mm(get(dp, h, e), wq[dq.weight(h, e)], NT))

    def m_2():
        kept["m"] = small2(kept["m"], pkg, m1, ms1, m2)

    def m_3():
        kept["m"] = small3(kept["m"], ms1, m2, ms2, m3)

    def m_4():
        kept["m"] = small4(kept["m"], ms2, m3, kgp)

    def m_5():
        kept["m"] = small5(kept["m"], kgp)

    def k_1():
        local_done(wkv_l, wkv)
        kv = mm(tall(tpan), wkv[...], NN)
        for h in both:
            put(pkv, h, None, kv[:, h * HD:(h + 1) * HD])
        kept["k"] = small1(pkv, k1)

    def k_2():
        kept["k"] = small2(kept["k"], pkv, k1, ks1, k2)

    def k_3():
        kept["k"] = small3(kept["k"], ks1, k2, ks2, k3)

    def k_4():
        kept["k"] = small4(kept["k"], ks2, k3, kvp)

    def k_5():
        kept["k"] = small5(kept["k"], kvp)

    compute(0)
    start(0)
    k_1()
    compute(1)
    start(1)
    compute(2)
    start(2)
    relay(0)
    k_2()
    compute(3)
    start(3)
    relay(1)
    collect(0)
    k_3()
    g_ready()
    compute(4)
    start(4)
    relay(2)
    collect(1)
    across(0)
    k_4()
    compute(5)
    start(5)
    relay(3)
    collect(2)
    across(1)
    k_5()
    compute(6)
    start(6)
    collect(3)
    relay(4)
    across(2)
    compute(7)
    start(7)
    across(3)
    relay(5)
    collect(4)
    relay(6)
    collect(5)
    across(4)
    relay(7)
    forward()
    att.start()
    att.across(0)
    collect(6)
    across(5)
    collect(7)
    att.across(1)
    across(6)
    att.ring(0)
    att.across(2)
    across(7)
    att.across(3)
    att.ring(1)
    backward()
    att.ring(2)
    att.relay(0)
    att.ring(3)
    m_2()
    att.relay(1)
    dq.across(1)
    dq.across(2)
    dq.ring(0)
    m_3()
    dq.across(3)
    dq.ring(1)
    att.relay(2)
    m_4()
    dq.ring(2)
    att.relay(3)
    dq.relay(0)
    dq.ring(3)
    m_5()
    dq.relay(1)
    att.done(0)
    output_part(0)
    att.done(1)
    output_part(1)
    dq.relay(2)
    att.done(2)
    output_part(2)
    att.done(3)
    output_part(3)
    dq.relay(3)
    output_send()
    tokens_t[...] = tall(tpan).T
    kv_grad_part()
    dq.done(0)
    token_grad_part(0)
    dq.done(1)
    token_grad_part(1)
    dq.done(2)
    token_grad_part(2)
    dq.done(3)
    token_grad_part(3)
    t_part[...] = acc[...].astype(BF16).reshape(N, part_rows, -1)
    kept["t"] = fan("n", lambda i: t_part.at[i], lambda d: t_recv.at[d - 1], t_recv)
    w_output_grad(0)
    w_output_grad(1)
    w_output_grad(2)
    w_output_grad(3)
    output_end()
    w_query_grad(0)
    w_query_grad(1)
    w_query_grad(2)
    w_query_grad(3)

    got(*kept["t"])
    sum_narrow(t_part, t_recv, t_out)
    store([(t_out, gtok_h)], t_out)
    for sem, ref in stores:
        local_done(sem, ref)
    for n in range(max(0, len(sends) - SEND_SEMS), len(sends)):
        wait_sent(n)


def last_kernel(*refs):
    loads = []
    for src, held, dst in zip(refs[:5], refs[10:15], refs[5:10]):
        n = PIECES if src.shape[0] * src.shape[1] > 2 ** 18 else 1
        size = src.shape[0] // n
        for i in range(n):
            at = slice(i * size, (i + 1) * size)
            c = pltpu.make_async_copy(src.at[at], held.at[at], refs[15].at[len(loads)])
            c.start()
            loads.append((c, held.at[at], dst.at[at]))
    stores = []
    for c, src, dst in loads:
        c.wait()
        stores.append(pltpu.make_async_copy(src, dst, refs[16].at[len(stores)]))
        stores[-1].start()
    for c in stores:
        c.wait()


def shards(K, N, tokens, w_query, w_keyval, w_output, grad_out):
    part_rows, feat = tokens.shape
    rows = part_rows * N
    R = rows // (K * K)
    qc = w_query.shape[1]
    Z = K
    C = 2 * Z
    U = qc // C
    B = K // 2
    assert w_keyval.shape[1] == 2 * HD and U % HD == 0 and N == 4 and K == 4

    def v(*shape):
        return pltpu.VMEM(shape, BF16)

    def reduce_buffers():
        return [
            v(2, 2, K, B, R, U), v(2, 2, K, B, R, U), v(2, 2, K, K, R, U), v(2, K, K, R, U),
            v(2, K - 1, K, R, U), v(2, K, R, U), v(K - 1, 2, R, U), v(2, R, U),
        ]

    def pair_buffers():
        return [
            v(2, K - 1, K, R, HD), v(2, K, R, HD), v(2, K - 1, R, HD), v(2, R, HD),
            v(2, K - 1, R, HD),
        ]

    def panel():
        return v(2, K, K, K, R, U)

    def pair_panel():
        return v(2, K, K, R, HD)

    scratch = (
        [v(C, feat, U), v(*w_keyval.shape), v(*w_output.shape)]
        + [v(N, part_rows, feat), v(N, part_rows, feat)]
        + [panel(), panel(), pair_panel(), pair_panel()]
        + reduce_buffers() + reduce_buffers() + pair_buffers() + pair_buffers()
        + [pair_panel(), pair_panel(), v(rows, 2 * HD), panel(), panel()]
        + [pltpu.VMEM((rows, feat), F32)]
        + [v(N, part_rows, feat), v(N - 1, part_rows, feat)] * 2
        + [v(part_rows, feat), v(part_rows, feat)]
        + [v(feat, rows), v(2, K, feat, U), v(*w_keyval.shape), v(2, K, U, feat)]
        + [pltpu.SemaphoreType.DMA((SEND_SEMS,)), pltpu.SemaphoreType.DMA((RECV_SEMS,))]
        + [pltpu.SemaphoreType.DMA((LOCAL_SEMS,))]
    )
    anywhere = pl.BlockSpec(memory_space=pl.ANY)

    def array(*shape):
        return jax.ShapeDtypeStruct(shape, BF16)

    shapes = (
        array(part_rows, feat), array(part_rows, feat),
        array(feat, qc), array(feat, 2 * HD), array(qc, feat),
    )
    results = pl.pallas_call(
        functools.partial(kernel, K, N),
        out_shape=shapes,
        in_specs=[anywhere] * 5,
        out_specs=(anywhere,) * 5,
        scratch_shapes=scratch,
        compiler_params=pltpu.CompilerParams(
            collective_id=0, has_side_effects=True, vmem_limit_bytes=56 * 1024 * 1024
        ),
        name="layer",
    )(tokens, w_query, w_keyval, w_output, grad_out)
    return pl.pallas_call(
        last_kernel,
        out_shape=shapes,
        in_specs=[anywhere] * 5,
        out_specs=(anywhere,) * 5,
        scratch_shapes=[v(*s.shape) for s in shapes]
        + [pltpu.SemaphoreType.DMA((3 + 2 * PIECES,))] * 2,
        compiler_params=pltpu.CompilerParams(vmem_limit_bytes=60 * 1024 * 1024),
        name="hand_over",
    )(*results)


def solution(mesh):
    N, wide = mesh.shape["narrow"], mesh.shape["wide"]
    K = next(k for k in range(1, wide + 1) if k ** 3 >= wide)
    assert K ** 3 == wide
    return jax.shard_map(
        functools.partial(shards, K, N),
        mesh=mesh,
        in_specs=(
            P("narrow", "wide"),
            P("wide", "narrow"),
            P("wide", "narrow"),
            P("narrow", "wide"),
            P("narrow", "wide"),
        ),
        out_specs=(
            P("narrow", "wide"),
            P("narrow", "wide"),
            P("wide", "narrow"),
            P("wide", "narrow"),
            P("narrow", "wide"),
        ),
        check_vma=False,
    )
```

```python
import functools

import jax
import jax.numpy as jnp
from jax import lax
from jax.experimental import pallas as pl
from jax.experimental.pallas import tpu as pltpu
from jax.sharding import PartitionSpec as P

HD = 128
F32 = jnp.float32
BF16 = jnp.bfloat16
MESH = pl.DeviceIdType.MESH
RECV_SEMS = 130
SEND_SEMS = 32
LOCAL_SEMS = 24
PIECES = 4
REDUCE_GROUPS = ((0, 1), (1, 2), (2, 3), (3, 4))
GATHER_GROUPS = ((0, 1), (1, 2), (2, 3), (3, 4))


def mm(left, right, dims):
    return lax.dot_general(left, right, (dims, ((), ())), preferred_element_type=F32)


NN = ((1,), (0,))
NT = ((1,), (1,))
TN = ((0,), (0,))


def kernel(
    K, N, tok, wq_h, wkv_h, wo_h, gout,
    out_h, gtok_h, gwq_h, gwkv_h, gwo_h,
    wq, wkv, wo, tpan, gpan, pq, pg, pkv, pkg,
    q_far, q_mid, q_near, qs1, q2, qs2, q3, qf,
    g_far, g_mid, g_near, gs1, g2, gs2, g3, gf,
    k1, ks1, k2, ks2, k3,
    m1, ms1, m2, ms2, m3,
    kvp, kgp, kg, ap, dp, acc, o_part, o_recv, t_part, t_recv, o_out, t_out,
    tokens_t, gwq_o, gwkv_o, gwo_o,
    send_sems, recv_sems, local_sems,
):
    Z = K
    B = K // 2
    R, U = pq.shape[4], pq.shape[5]
    rows = K * K * R
    C = 2 * Z
    me = lax.axis_index("wide")
    nar = lax.axis_index("narrow")
    z, x, y = me // (K * K), (me // K) % K, me % K
    part_rows = rows // N
    both = (0, 1)
    first = ("x", "y")
    second = ("y", "x")
    spot = (x, y)
    low, high = slice(0, B), slice(B, K)

    def peer(axis, d):
        if axis == "core":
            i = nar + 1 - 2 * (nar % 2)
            return {"narrow": i}, i
        if axis == "n":
            i = (nar + d) % N
            return {"narrow": i}, i
        if axis == "z":
            i = (z + d) % K
            return {"wide": i * K * K + x * K + y}, i
        if axis == "x":
            i = (x + d) % K
            return {"wide": z * K * K + i * K + y}, i
        i = (y + d) % K
        return {"wide": z * K * K + x * K + i}, i

    count = [0]
    sends = []

    def receiver():
        count[0] += 1
        return count[0] - 1

    def remote(axis, d, src, dst, send_sem, recv_sem):
        return pltpu.make_async_remote_copy(
            src_ref=src, dst_ref=dst, send_sem=send_sems.at[send_sem],
            recv_sem=recv_sems.at[recv_sem], device_id=peer(axis, d)[0], device_id_type=MESH,
        )

    def wait_sent(n):
        i, ref = sends[n]
        remote("core", 1, ref, ref, i, 0).wait_send()

    def batch(items, gone):
        n = len(sends)
        if n >= SEND_SEMS:
            wait_sent(n - SEND_SEMS)
        i = n % SEND_SEMS
        sends.append((i, gone))
        for axis, d, src, dst, r in items:
            remote(axis, d, src, dst, i, r).start()

    def got(r, ref):
        remote("core", 1, ref, ref, 0, r).wait_recv()

    def fan(axis, src, dst, whole):
        r = receiver()
        ds = range(1, N if axis == "n" else K)
        batch([(axis, d, src(peer(axis, d)[1]), dst(d), r) for d in ds], whole)
        return r, whole

    locals_used = [0]

    def local(pairs):
        sem = local_sems.at[locals_used[0]]
        locals_used[0] += 1
        for s, d in pairs:
            pltpu.make_async_copy(s, d, sem).start()
        return sem

    def local_done(sem, ref):
        pltpu.make_async_copy(ref, ref, sem).wait()

    tok_l = local([(tok, tpan.at[nar])])
    gout_l = local([(gout, gpan.at[nar])])
    wkv_l = local([(wkv_h, wkv)])
    wq_l = local([(wq_h.at[:, c * U:(c + 1) * U], wq.at[c]) for c in range(C)])
    wo_l = local([(wo_h, wo)])

    barrier = pltpu.get_barrier_semaphore()
    peers = [("n", d) for d in range(1, N)] + [(a, d) for a in "zxy" for d in range(1, K)]
    for a, d in peers:
        pl.semaphore_signal(barrier, inc=1, device_id=peer(a, d)[0], device_id_type=MESH)
    pl.semaphore_wait(barrier, len(peers))

    def share_start(own, pan):
        far, near = receiver(), receiver()
        batch(
            [("n", 2, own, pan.at[nar], far), ("core", 1, own, pan.at[nar], near)], pan.at[0:2]
        )
        return far, near

    def share_end(pan, far, near):
        other = (nar + 2) % N
        got(far, pan.at[0])
        batch([("core", 1, pan.at[other], pan.at[other], near)], pan.at[0])
        got(near, pan.at[0:2])

    tok_c = share_start(tok, tpan)
    gout_c = share_start(gout, gpan)

    def put(p, h, e, v):
        v = v.astype(BF16).reshape(K, K, R, -1)
        at = (h,) if e is None else (h, e)
        if h == 0:
            p[at] = v
        else:
            for i in range(K):
                p[at + (slice(0, K), i)] = v[i]

    def get(p, h, e):
        at = (h,) if e is None else (h, e)
        if h == 0:
            return p[at].reshape(rows, -1)
        return jnp.concatenate(
            [p[at + (slice(0, K), i)].reshape(K * R, -1) for i in range(K)], axis=0
        )

    def small1(p, recv):
        out = []
        for h in both:
            out.append(fan(first[h], lambda i: p.at[h, i], lambda d: recv.at[h, d - 1], recv.at[h]))
        return out

    def small2(waits, p, recv, s, recv2):
        out = []
        for h in both:
            got(*waits[h])
            total = p[h, spot[h]].astype(F32)
            for d in range(K - 1):
                total += recv[h, d].astype(F32)
            s[h] = total.astype(BF16)
            out.append(fan(second[h], lambda i: s.at[h, i], lambda d: recv2.at[h, d - 1], recv2.at[h]))
        return out

    def small3(waits, s, recv2, t, recv3):
        out = []
        for h in both:
            got(*waits[h])
            total = s[h, spot[1 - h]].astype(F32)
            for d in range(K - 1):
                total += recv2[h, d].astype(F32)
            t[h] = total.astype(BF16)
            out.append(fan("z", lambda i: t.at[h], lambda d: recv3.at[h, d - 1], recv3.at[h]))
        return out

    def small4(waits, t, recv3, p):
        out = []
        for h in both:
            got(*waits[h])
            total = t[h].astype(F32)
            for d in range(K - 1):
                total += recv3[h, d].astype(F32)
            p[h, spot[h], spot[1 - h]] = total.astype(BF16)
            here = p.at[h, spot[h], spot[1 - h]]
            out.append(fan(second[h], lambda i: here, lambda d: here, p.at[h, 0, 1:K]))
        return out

    def small5(waits, p):
        out = []
        for h in both:
            got(*waits[h])
            here = p.at[h, spot[h]]
            out.append(fan(first[h], lambda i: here, lambda d: here, p.at[h, 1:K]))
        return out

    def view(h, slots, i, part):
        return (h, slots, i, part)

    class Reduce:
        groups = REDUCE_GROUPS

        def __init__(self, p, far, mid, near, s1, r2, s2, r3, f):
            self.p, self.far, self.mid, self.near = p, far, mid, near
            self.s1, self.r2, self.s2, self.r3, self.f = s1, r2, s2, r3, f
            self.c1, self.c2 = {}, {}
            self.c3 = receiver()

        def weight(self, h, e):
            return h * Z + (z + 1 + e) % K

        def start(self, n):
            slots = slice(*self.groups[n])
            for h in both:
                i = spot[h]
                there, after, before = (i + 2) % K, (i + 1) % K, (i + K - 1) % K
                axis, p = first[h], self.p
                f, r = receiver(), receiver()
                self.c1[n, h] = f, r
                batch([
                    (axis, 1, p.at[view(h, slots, there, low)], self.far.at[h, 0, slots], f),
                    (axis, K - 1, p.at[view(h, slots, there, high)], self.far.at[h, 1, slots], f),
                    (axis, 1, p.at[view(h, slots, after, high)], self.near.at[h, 0, slots, high], r),
                    (axis, K - 1, p.at[view(h, slots, before, low)], self.near.at[h, 1, slots, low], r),
                ], self.near.at[h, :, slots])

        def relay(self, n):
            slots = slice(*self.groups[n])
            for h in both:
                i = spot[h]
                f, r = self.c1[n, h]
                got(f, self.far.at[h, :, slots])
                items = []
                for side, d, part in ((0, 1, low), (1, K - 1, high)):
                    for e in range(*self.groups[n]):
                        own = self.p[view(h, e, (i + d) % K, part)].astype(F32)
                        total = own + self.far[h, side, e].astype(F32)
                        self.mid[h, side, e] = total.astype(BF16)
                    items.append((
                        first[h], d, self.mid.at[h, side, slots],
                        self.near.at[h, side, slots, part], r,
                    ))
                batch(items, self.mid.at[h, :, slots])

        def collect(self, n):
            slots = slice(*self.groups[n])
            for h in both:
                got(self.c1[n, h][1], self.near.at[h, :, slots])
                for e in range(*self.groups[n]):
                    total = self.p[view(h, e, spot[h], slice(0, K))].astype(F32)
                    total += self.near[h, 0, e].astype(F32)
                    total += self.near[h, 1, e].astype(F32)
                    self.s1[h, e] = total.astype(BF16)
                self.c2[n, h] = fan(
                    second[h], lambda i: self.s1.at[h, slots, i],
                    lambda d: self.r2.at[h, d - 1, slots], self.r2.at[h, :, slots],
                )

        def across(self, n):
            for h in both:
                got(*self.c2[n, h])
                for e in range(*self.groups[n]):
                    total = self.s1[h, e, spot[1 - h]].astype(F32)
                    for d in range(K - 1):
                        total += self.r2[h, d, e].astype(F32)
                    self.s2[h, e] = total.astype(BF16)
            items = [
                ("z", e + 1, self.s2.at[:, e], self.r3.at[e], self.c3)
                for e in range(*self.groups[n]) if e < K - 1
            ]
            if items:
                batch(items, self.r3.at[0:len(items)])

        def finish(self):
            got(self.c3, self.r3)
            total = self.s2[:, K - 1].astype(F32)
            for d in range(K - 1):
                total += self.r3[d].astype(F32)
            self.f[...] = total.astype(BF16)

    class Gather:
        groups = GATHER_GROUPS

        def __init__(self, p):
            self.p = p
            self.c1, self.c2, self.c3, self.c4 = [], {}, {}, {}

        def weight(self, h, e):
            return h * Z + (z + K - e) % K

        def start(self):
            p = self.p
            self.c1 = [receiver() for d in range(1, K)]
            batch(
                [
                    ("z", d, p.at[h, 0, spot[h], spot[1 - h]], p.at[h, d, spot[h], spot[1 - h]],
                     self.c1[d - 1])
                    for d in range(1, K) for h in both
                ],
                p.at[:, 1:K, 0, 0],
            )

        def across(self, n):
            e0, e1 = self.groups[n]
            for e in range(max(e0, 1), e1):
                got(self.c1[e - 1], self.p.at[:, e, 0, 0])
            for h in both:
                here = self.p.at[h, e0:e1, spot[h], spot[1 - h]]
                self.c2[n, h] = fan(
                    second[h], lambda i: here, lambda d: here, self.p.at[h, e0:e1, 0, 1:K]
                )

        def ring(self, n):
            slots = slice(*self.groups[n])
            for h in both:
                got(*self.c2[n, h])
                here = self.p.at[view(h, slots, spot[h], slice(0, K))]
                r = receiver()
                self.c3[n, h] = r
                batch([(first[h], d, here, here, r) for d in (1, K - 1)], self.p.at[h, slots, 0:2])

        def relay(self, n):
            slots = slice(*self.groups[n])
            for h in both:
                got(self.c3[n, h], self.p.at[h, slots, 0:2])
                r = receiver()
                self.c4[n, h] = r
                items = []
                for d, part in ((1, low), (K - 1, high)):
                    here = self.p.at[view(h, slots, (spot[h] + K - d) % K, part)]
                    items.append((first[h], d, here, here, r))
                batch(items, self.p.at[h, slots, 0])

        def done(self, n):
            slots = slice(*self.groups[n])
            for h in both:
                got(self.c4[n, h], self.p.at[h, slots, 0])

    def tall(pan):
        return pan[...].reshape(rows, -1)

    local_done(tok_l, tok)
    share_end(tpan, *tok_c)
    local_done(wq_l, wq)

    q = Reduce(pq, q_far, q_mid, q_near, qs1, q2, qs2, q3, qf)
    g = Reduce(pg, g_far, g_mid, g_near, gs1, g2, gs2, g3, gf)

    def project(n):
        for e in range(*q.groups[n]):
            for h in both:
                put(pq, h, e, mm(tall(tpan), wq[q.weight(h, e)], NN))

    def back_out(n):
        for e in range(*g.groups[n]):
            for h in both:
                at = pl.multiple_of(g.weight(h, e) * U, U)
                put(pg, h, e, mm(tall(gpan), wo[pl.ds(at, U), :], NT))

    G = len(REDUCE_GROUPS)
    work = [(q, n) for n in range(G)] + [(g, n) for n in range(G)]

    def compute(t):
        s, n = work[t]
        (project if s is q else back_out)(n)

    def start(t):
        work[t][0].start(work[t][1])

    def relay(t):
        work[t][0].relay(work[t][1])

    def collect(t):
        work[t][0].collect(work[t][1])

    def across(t):
        work[t][0].across(work[t][1])

    def g_ready():
        share_end(gpan, *gout_c)
        local_done(gout_l, gout)
        local_done(wo_l, wo)

    def heads(f):
        return jnp.concatenate(
            [f[h, :, k * HD:(k + 1) * HD] for h in both for k in range(U // HD)], axis=0
        )

    def unheads(p, v):
        per = U // HD
        for h in both:
            p[h, 0, spot[h], spot[1 - h]] = jnp.concatenate(
                [v[(h * per + k) * R:(h * per + k + 1) * R] for k in range(per)], axis=1
            )

    scale = HD ** (-0.5)
    kept = {}

    def output_end():
        got(*kept["o"])
        sum_narrow(o_part, o_recv, o_out)
        store([(o_out, out_h)], o_out)

    def forward():
        q.finish()
        for h in both:
            got(*kept["k"][h])
        queries = heads(qf)
        keys = get(kvp, 0, None)
        values = get(kvp, 1, None)
        scores = mm(queries, keys, NT) * scale
        place = lax.broadcasted_iota(jnp.int32, scores.shape, 0) % R + (x * K + y) * R
        allowed = lax.broadcasted_iota(jnp.int32, scores.shape, 1) <= place
        weights = jnp.where(allowed, jnp.exp(scores), 0.0)
        weights = weights / jnp.sum(weights, axis=1, keepdims=True)
        probs = weights.astype(BF16)
        unheads(ap, mm(probs, values, NN).astype(BF16))
        kept["fwd"] = queries, keys, values, weights, probs

    def backward():
        g.finish()
        queries, keys, values, weights, probs = kept["fwd"]
        cotangent = heads(gf)
        prob_grad = mm(cotangent, values, NT)
        score_grad = weights * (prob_grad - jnp.sum(weights * prob_grad, axis=1, keepdims=True))
        score_half = score_grad.astype(BF16)
        unheads(dp, (mm(score_half, keys, NN) * scale).astype(BF16))
        dq.start()
        dq.across(0)
        grad_keys = mm(score_half, queries, TN) * scale
        grad_values = mm(probs, cotangent, TN)
        put(pkg, 0, None, grad_keys)
        put(pkg, 1, None, grad_values)
        kept["m"] = small1(pkg, m1)

    att = Gather(ap)
    dq = Gather(dp)
    stores = []

    def store(pairs, ref):
        stores.append((local(pairs), ref))

    def sum_narrow(part, recv, o):
        total = part[nar].astype(F32)
        for d in range(N - 1):
            total += recv[d].astype(F32)
        o[...] = total.astype(BF16)

    def w_output_grad(n):
        for e in range(*att.groups[n]):
            for h in both:
                c = att.weight(h, e)
                gwo_o[h, e] = mm(get(ap, h, e), tall(gpan), TN).astype(BF16)
                store([(gwo_o.at[h, e], gwo_h.at[pl.ds(pl.multiple_of(c * U, U), U), :])], gwo_o.at[h, e])

    def w_query_grad(n):
        for e in range(*dq.groups[n]):
            for h in both:
                c = dq.weight(h, e)
                gwq_o[h, e] = mm(tokens_t[...], get(dp, h, e), NN).astype(BF16)
                store([(gwq_o.at[h, e], gwq_h.at[:, pl.ds(pl.multiple_of(c * U, U), U)])], gwq_o.at[h, e])

    def add(term, start=False):
        acc[...] = term if start else acc[...] + term

    def output_part(n):
        for e in range(*att.groups[n]):
            for h in both:
                at = pl.multiple_of(att.weight(h, e) * U, U)
                add(mm(get(ap, h, e), wo[pl.ds(at, U), :], NN), e == 0 and h == 0)

    def output_send():
        o_part[...] = acc[...].astype(BF16).reshape(N, part_rows, -1)
        kept["o"] = fan("n", lambda i: o_part.at[i], lambda d: o_recv.at[d - 1], o_recv)

    def kv_grad_part():
        for h in both:
            got(*kept["m"][h])
        kg[...] = jnp.concatenate([get(kgp, h, None) for h in both], axis=1)
        gwkv_o[...] = mm(tokens_t[...], kg[...], NN).astype(BF16)
        store([(gwkv_o, gwkv_h)], gwkv_o)
        add(mm(kg[...], wkv[...], NT), True)

    def token_grad_part(n):
        for e in range(*dq.groups[n]):
            for h in both:
                add(mm(get(dp, h, e), wq[dq.weight(h, e)], NT))

    def m_2():
        kept["m"] = small2(kept["m"], pkg, m1, ms1, m2)

    def m_3():
        kept["m"] = small3(kept["m"], ms1, m2, ms2, m3)

    def m_4():
        kept["m"] = small4(kept["m"], ms2, m3, kgp)

    def m_5():
        kept["m"] = small5(kept["m"], kgp)

    def k_1():
        local_done(wkv_l, wkv)
        kv = mm(tall(tpan), wkv[...], NN)
        for h in both:
            put(pkv, h, None, kv[:, h * HD:(h + 1) * HD])
        kept["k"] = small1(pkv, k1)

    def k_2():
        kept["k"] = small2(kept["k"], pkv, k1, ks1, k2)

    def k_3():
        kept["k"] = small3(kept["k"], ks1, k2, ks2, k3)

    def k_4():
        kept["k"] = small4(kept["k"], ks2, k3, kvp)

    def k_5():
        kept["k"] = small5(kept["k"], kvp)

    compute(0)
    start(0)
    k_1()
    compute(1)
    start(1)
    compute(2)
    start(2)
    relay(0)
    k_2()
    compute(3)
    start(3)
    relay(1)
    collect(0)
    k_3()
    g_ready()
    compute(4)
    start(4)
    relay(2)
    collect(1)
    across(0)
    k_4()
    compute(5)
    start(5)
    relay(3)
    collect(2)
    across(1)
    k_5()
    compute(6)
    start(6)
    collect(3)
    relay(4)
    across(2)
    compute(7)
    start(7)
    across(3)
    relay(5)
    collect(4)
    relay(6)
    collect(5)
    across(4)
    relay(7)
    forward()
    att.start()
    att.across(0)
    collect(6)
    across(5)
    collect(7)
    att.across(1)
    across(6)
    att.ring(0)
    att.across(2)
    across(7)
    att.across(3)
    att.ring(1)
    backward()
    att.ring(2)
    att.relay(0)
    att.ring(3)
    m_2()
    att.relay(1)
    dq.across(1)
    dq.across(2)
    dq.ring(0)
    m_3()
    dq.across(3)
    dq.ring(1)
    att.relay(2)
    m_4()
    dq.ring(2)
    att.relay(3)
    dq.relay(0)
    dq.ring(3)
    m_5()
    dq.relay(1)
    att.done(0)
    output_part(0)
    att.done(1)
    output_part(1)
    dq.relay(2)
    att.done(2)
    output_part(2)
    att.done(3)
    output_part(3)
    dq.relay(3)
    output_send()
    tokens_t[...] = tall(tpan).T
    kv_grad_part()
    dq.done(0)
    token_grad_part(0)
    dq.done(1)
    token_grad_part(1)
    dq.done(2)
    token_grad_part(2)
    dq.done(3)
    token_grad_part(3)
    t_part[...] = acc[...].astype(BF16).reshape(N, part_rows, -1)
    kept["t"] = fan("n", lambda i: t_part.at[i], lambda d: t_recv.at[d - 1], t_recv)
    w_output_grad(0)
    w_output_grad(1)
    w_output_grad(2)
    w_output_grad(3)
    output_end()
    w_query_grad(0)
    w_query_grad(1)
    w_query_grad(2)
    w_query_grad(3)

    got(*kept["t"])
    sum_narrow(t_part, t_recv, t_out)
    store([(t_out, gtok_h)], t_out)
    for sem, ref in stores:
        local_done(sem, ref)
    for n in range(max(0, len(sends) - SEND_SEMS), len(sends)):
        wait_sent(n)


def last_kernel(*refs):
    loads = []
    for src, held, dst in zip(refs[:5], refs[10:15], refs[5:10]):
        n = PIECES if src.shape[0] * src.shape[1] > 2 ** 18 else 1
        size = src.shape[0] // n
        for i in range(n):
            at = slice(i * size, (i + 1) * size)
            c = pltpu.make_async_copy(src.at[at], held.at[at], refs[15].at[len(loads)])
            c.start()
            loads.append((c, held.at[at], dst.at[at]))
    stores = []
    for c, src, dst in loads:
        c.wait()
        stores.append(pltpu.make_async_copy(src, dst, refs[16].at[len(stores)]))
        stores[-1].start()
    for c in stores:
        c.wait()


def shards(K, N, tokens, w_query, w_keyval, w_output, grad_out):
    part_rows, feat = tokens.shape
    rows = part_rows * N
    R = rows // (K * K)
    qc = w_query.shape[1]
    Z = K
    C = 2 * Z
    U = qc // C
    B = K // 2
    assert w_keyval.shape[1] == 2 * HD and U % HD == 0 and N == 4 and K == 4

    def v(*shape):
        return pltpu.VMEM(shape, BF16)

    def reduce_buffers():
        return [
            v(2, 2, K, B, R, U), v(2, 2, K, B, R, U), v(2, 2, K, K, R, U), v(2, K, K, R, U),
            v(2, K - 1, K, R, U), v(2, K, R, U), v(K - 1, 2, R, U), v(2, R, U),
        ]

    def pair_buffers():
        return [
            v(2, K - 1, K, R, HD), v(2, K, R, HD), v(2, K - 1, R, HD), v(2, R, HD),
            v(2, K - 1, R, HD),
        ]

    def panel():
        return v(2, K, K, K, R, U)

    def pair_panel():
        return v(2, K, K, R, HD)

    scratch = (
        [v(C, feat, U), v(*w_keyval.shape), v(*w_output.shape)]
        + [v(N, part_rows, feat), v(N, part_rows, feat)]
        + [panel(), panel(), pair_panel(), pair_panel()]
        + reduce_buffers() + reduce_buffers() + pair_buffers() + pair_buffers()
        + [pair_panel(), pair_panel(), v(rows, 2 * HD), panel(), panel()]
        + [pltpu.VMEM((rows, feat), F32)]
        + [v(N, part_rows, feat), v(N - 1, part_rows, feat)] * 2
        + [v(part_rows, feat), v(part_rows, feat)]
        + [v(feat, rows), v(2, K, feat, U), v(*w_keyval.shape), v(2, K, U, feat)]
        + [pltpu.SemaphoreType.DMA((SEND_SEMS,)), pltpu.SemaphoreType.DMA((RECV_SEMS,))]
        + [pltpu.SemaphoreType.DMA((LOCAL_SEMS,))]
    )
    anywhere = pl.BlockSpec(memory_space=pl.ANY)

    def array(*shape):
        return jax.ShapeDtypeStruct(shape, BF16)

    shapes = (
        array(part_rows, feat), array(part_rows, feat),
        array(feat, qc), array(feat, 2 * HD), array(qc, feat),
    )
    results = pl.pallas_call(
        functools.partial(kernel, K, N),
        out_shape=shapes,
        in_specs=[anywhere] * 5,
        out_specs=(anywhere,) * 5,
        scratch_shapes=scratch,
        compiler_params=pltpu.CompilerParams(
            collective_id=0, has_side_effects=True, vmem_limit_bytes=56 * 1024 * 1024
        ),
        name="layer",
    )(tokens, w_query, w_keyval, w_output, grad_out)
    return pl.pallas_call(
        last_kernel,
        out_shape=shapes,
        in_specs=[anywhere] * 5,
        out_specs=(anywhere,) * 5,
        scratch_shapes=[v(*s.shape) for s in shapes]
        + [pltpu.SemaphoreType.DMA((3 + 2 * PIECES,))] * 2,
        compiler_params=pltpu.CompilerParams(vmem_limit_bytes=60 * 1024 * 1024),
        name="hand_over",
    )(*results)


def solution(mesh):
    N, wide = mesh.shape["narrow"], mesh.shape["wide"]
    K = next(k for k in range(1, wide + 1) if k ** 3 >= wide)
    assert K ** 3 == wide
    return jax.shard_map(
        functools.partial(shards, K, N),
        mesh=mesh,
        in_specs=(
            P("narrow", "wide"),
            P("wide", "narrow"),
            P("wide", "narrow"),
            P("narrow", "wide"),
            P("narrow", "wide"),
        ),
        out_specs=(
            P("narrow", "wide"),
            P("narrow", "wide"),
            P("wide", "narrow"),
            P("wide", "narrow"),
            P("narrow", "wide"),
        ),
        check_vma=False,
    )
```
